256 devices in a mesh: seq: 16 (over y, x), row: 4 (over z_hi), col: 4 (over z_lo, core).
Axes of the slice: x: 4, y: 4, z: 8 (z_hi: 4, z_lo: 2; z = z_hi * 2 + z_lo), core: 2. Of those that a mesh axis runs over, the one named last changes fastest.
Arguments:
- alignment_input: bfloat16 [512, 256, 64], P('seq', ('row', 'col')), may hold values from -30 to 30
- pair_input: bfloat16 [256, 256, 128], P('row', 'col'), may hold values from -60 to 60
- token_valid_mask: int32 [256], replicated, may hold values from 0 to 1, as said below
- first_factor_weights: bfloat16 [64, 32], replicated, may hold values from -0.75 to 0.75
- second_factor_weights: bfloat16 [64, 32], replicated, may hold values from -0.75 to 0.75
- content_weights_grid: bfloat16 [64, 256], replicated, may hold values from -0.75 to 0.75
- sigmoid_weights_grid: bfloat16 [64, 256], replicated, may hold values from -0.75 to 0.75
- outer_matrix: float32 [1024, 128], replicated, may hold values from -0.0078125 to 0.0078125
- score_matrix: float32 [128, 8], replicated, may hold values from -20 to 20
- final_mixing_weights: bfloat16 [256, 64], replicated, may hold values from -0.375 to 0.375
- adjoint_of_rowset: bfloat16 [512, 256, 64], P('seq', ('row', 'col')), may hold values from -48 to 48
Outputs:
- alignment_output: bfloat16 [512, 256, 64], P('seq', ('row', 'col'))
- pair_output: bfloat16 [256, 256, 128], P('row', 'col')
- pair_gradient: bfloat16 [256, 256, 128], P('row', 'col')
The draws below stay inside these ranges and needn't reach their ends.
Inputs may be any that keep to these rules, and one draw needn't show every extreme that they name: `token_valid_mask`: the mask is 1 on a first run of more than half of the 256 tokens and 0 on the rest.
All inputs are finite; a program needn't handle non-finite values.
Results may differ from the reference program's by a relative error of at most 0.028.
The reference program's roundings to bfloat16 on the way count: a program that leaves them out, or rounds other values in their place, can miss the bound.
Values may be sent and summed in bfloat16 or wider, within the bound.
A program may use at most 64 MiB of HBM per device.

```python
import math
import jax
import jax.numpy as jnp
from jax import lax

FEATURE_WIDTH = 64
CZ = 128
FACTOR_WIDTH = 32
ATTENTION_HEADS = 8
HEAD_WIDTH = 32
ROW_TOTAL_NUM = 512
RESIDUE_NUMBER = 256


def score_base(key):
    return jax.random.normal(jax.random.fold_in(key, 101), (CZ, ATTENTION_HEADS), jnp.float32)


def draw_score_matrix(key, part):
    base = score_base(key)
    key = jax.random.fold_in(key, 7)
    head_scale = jnp.exp(jax.random.uniform(key, (1, ATTENTION_HEADS), jnp.float32, math.log(0.6), math.log(2.4)))
    return base * head_scale / math.sqrt(CZ)


def draw_pair_input(key, part):
    key = jax.random.fold_in(key, 11)
    perturbation_seed, multiplier_seed = jax.random.split(key, 2)
    feature_multiplier = jnp.exp(jax.random.uniform(multiplier_seed, (CZ,), jnp.float32, math.log(0.3), math.log(3.0)))
    random_perturbation = jax.random.normal(perturbation_seed, (RESIDUE_NUMBER, RESIDUE_NUMBER, CZ), jnp.float32)
    return (random_perturbation * feature_multiplier).astype(jnp.bfloat16)


def draw_alignment_input(key, part):
    key = jax.random.fold_in(key, 23)
    perturbation_seed, multiplier_seed = jax.random.split(key)
    feature_multiplier = jnp.exp(jax.random.uniform(multiplier_seed, (FEATURE_WIDTH,), jnp.float32, math.log(0.3), math.log(3.0)))
    random_perturbation = jax.random.normal(perturbation_seed, (ROW_TOTAL_NUM, RESIDUE_NUMBER, FEATURE_WIDTH), jnp.float32)
    return (random_perturbation * feature_multiplier).astype(jnp.bfloat16)


def draw_token_valid_mask(key, part):
    key = jax.random.fold_in(key, 31)
    length = jax.random.randint(key, (), RESIDUE_NUMBER // 2 + 1, RESIDUE_NUMBER + 1)
    return (jnp.arange(RESIDUE_NUMBER, dtype=jnp.int32) < length).astype(jnp.int32)


def level_of(rng, extent, pieces, least, high):
    def one(dim, blocks):
        draws = jax.random.uniform(jax.random.fold_in(jax.random.fold_in(rng, 6), dim), (blocks,), jnp.float32, least / len(pieces), high / len(pieces))
        return jnp.repeat(jnp.exp(draws), extent[dim] // blocks).reshape((-1,) + (1,) * (len(extent) - dim - 1))

    gain = one(*pieces[0])
    for cut in pieces[1:]:
        gain = gain * one(*cut)
    return gain


def noise(stream_key, shape, spread, limit, cuts=(), kind=jnp.bfloat16):
    drawn = spread * jax.random.normal(stream_key, shape, jnp.float32)
    if cuts:
        drawn = drawn * level_of(stream_key, shape, cuts, -0.22, 0.18)
    return jnp.clip(drawn, -limit, limit).astype(kind)


def setup_inputs(seed: int = 0) -> dict:
    splits = jax.random.split(jax.random.key(seed), 12)
    return {
        "alignment_input": draw_alignment_input(jax.random.fold_in(splits[11], 71), 0),
        "pair_input": draw_pair_input(jax.random.fold_in(splits[11], 71), 0),
        "token_valid_mask": draw_token_valid_mask(jax.random.fold_in(splits[11], 71), 0),
        "first_factor_weights": noise(splits[3], (FEATURE_WIDTH, FACTOR_WIDTH), FEATURE_WIDTH ** -0.5, 0.75),
        "second_factor_weights": noise(splits[4], (FEATURE_WIDTH, FACTOR_WIDTH), FEATURE_WIDTH ** -0.5, 0.75),
        "content_weights_grid": noise(splits[5], (FEATURE_WIDTH, ATTENTION_HEADS * HEAD_WIDTH), FEATURE_WIDTH ** -0.5, 0.75),
        "sigmoid_weights_grid": noise(splits[6], (FEATURE_WIDTH, ATTENTION_HEADS * HEAD_WIDTH), FEATURE_WIDTH ** -0.5, 0.75),
        "outer_matrix": noise(splits[7], (FACTOR_WIDTH * FACTOR_WIDTH, CZ), (FACTOR_WIDTH * FACTOR_WIDTH * ROW_TOTAL_NUM) ** -0.5, 0.0078125, (), jnp.float32),
        "score_matrix": draw_score_matrix(jax.random.fold_in(splits[11], 71), 0),
        "final_mixing_weights": noise(splits[9], (ATTENTION_HEADS * HEAD_WIDTH, FEATURE_WIDTH), (ATTENTION_HEADS * HEAD_WIDTH) ** -0.5, 0.375),
        "adjoint_of_rowset": noise(splits[10], (ROW_TOTAL_NUM, RESIDUE_NUMBER, FEATURE_WIDTH), 8.0, 48.0, ((0, 16), (1, 16))),
    }


epsilon = 1e-05
far_below = -1e+30

def layer_normalize(inputs):
    center = inputs - lax.optimization_barrier(jnp.mean(inputs, axis=-1, keepdims=True))
    inverse = lax.rsqrt(lax.optimization_barrier(jnp.mean(center * center, axis=-1, keepdims=True)) + epsilon)
    return (center * inverse, inverse)

def reference(alignment_input, pair_input, token_valid_mask, first_factor_weights, second_factor_weights, content_weights_grid, sigmoid_weights_grid, outer_matrix, score_matrix, final_mixing_weights, adjoint_of_rowset):
    highest = lax.Precision.HIGHEST
    mask_float = token_valid_mask.astype(jnp.float32)
    normalized_pair = layer_normalize(alignment_input.astype(jnp.float32))[0].astype(jnp.bfloat16)
    left_proj = (jnp.dot(normalized_pair, first_factor_weights, preferred_element_type=jnp.float32) * mask_float[None, :, None]).astype(jnp.bfloat16)
    right_proj = (jnp.dot(normalized_pair, second_factor_weights, preferred_element_type=jnp.float32) * mask_float[None, :, None]).astype(jnp.bfloat16)
    values = jnp.dot(normalized_pair, content_weights_grid, preferred_element_type=jnp.float32).astype(jnp.bfloat16)
    gating = jax.nn.sigmoid(jnp.dot(normalized_pair, sigmoid_weights_grid, preferred_element_type=jnp.float32))
    left_float = left_proj.astype(jnp.float32)
    right_float = right_proj.astype(jnp.float32)
    block_rows = math.gcd(RESIDUE_NUMBER, 16)

    def rows_update(number):
        row_start = (number * block_rows).astype(jnp.int32)
        rows_part = lax.dynamic_slice_in_dim(left_float, row_start, block_rows, 1)
        products = jnp.einsum('sic,sjd->ijcd', rows_part, right_float).reshape(block_rows, RESIDUE_NUMBER, FACTOR_WIDTH * FACTOR_WIDTH)
        return jnp.dot(products, outer_matrix, precision=highest, preferred_element_type=jnp.float32)
    update = lax.map(rows_update, jnp.arange(RESIDUE_NUMBER // block_rows, dtype=jnp.int32)).reshape(RESIDUE_NUMBER, RESIDUE_NUMBER, CZ)
    pair_output = (pair_input.astype(jnp.float32) + update).astype(jnp.bfloat16)
    normal_pair, inverse_pair = layer_normalize(pair_output.astype(jnp.float32))
    logits = jnp.dot(normal_pair, score_matrix, precision=highest, preferred_element_type=jnp.float32)
    valid_cols = mask_float[None, :, None] > 0
    masked = jnp.where(valid_cols, logits, far_below)
    row_max = lax.optimization_barrier(jnp.max(masked, axis=1, keepdims=True))
    scaled = jnp.exp(masked - row_max) * mask_float[None, :, None]
    probabilities = scaled / lax.optimization_barrier(jnp.sum(scaled, axis=1, keepdims=True))
    weights = probabilities.astype(jnp.bfloat16)
    head_values = values.astype(jnp.float32).reshape(ROW_TOTAL_NUM, RESIDUE_NUMBER, ATTENTION_HEADS, HEAD_WIDTH)
    averaged = jnp.einsum('ijh,sjhk->sihk', weights.astype(jnp.float32), head_values).reshape(ROW_TOTAL_NUM, RESIDUE_NUMBER, ATTENTION_HEADS * HEAD_WIDTH)
    gated_values = (gating * averaged).astype(jnp.bfloat16)
    alignment_output = (alignment_input.astype(jnp.float32) + jnp.dot(gated_values, final_mixing_weights, preferred_element_type=jnp.float32)).astype(jnp.bfloat16)
    gated_gradient = jnp.dot(adjoint_of_rowset, final_mixing_weights.T, preferred_element_type=jnp.float32)
    grad_avg = (gated_gradient * gating).astype(jnp.bfloat16)
    grad_heads = grad_avg.astype(jnp.float32).reshape(ROW_TOTAL_NUM, RESIDUE_NUMBER, ATTENTION_HEADS, HEAD_WIDTH)
    grad_weights = jnp.einsum('sihk,sjhk->ijh', grad_heads, head_values)
    inner_sum = lax.optimization_barrier(jnp.sum(probabilities * grad_weights, axis=1, keepdims=True))
    grad_logits = probabilities * (grad_weights - inner_sum)
    grad_normal = jnp.dot(grad_logits, score_matrix.T, precision=highest, preferred_element_type=jnp.float32)
    centered_grad = grad_normal - lax.optimization_barrier(jnp.mean(grad_normal, axis=-1, keepdims=True))
    along = lax.optimization_barrier(jnp.mean(grad_normal * normal_pair, axis=-1, keepdims=True))
    pair_gradient = (inverse_pair * (centered_grad - normal_pair * along)).astype(jnp.bfloat16)
    return (alignment_output, pair_output, pair_gradient)
```

```python
import jax
import jax.numpy as jnp
from jax import lax
from jax.experimental import pallas as pl
from jax.experimental.pallas import tpu as pltpu
from jax.sharding import PartitionSpec as P

F32 = jnp.float32
BF16 = jnp.bfloat16
I32 = jnp.int32
EPS = 1e-05
LOW = -1e30
MESH = pl.DeviceIdType.MESH

N = 16
NC = 4
TOK = 16
SEQ = 32
HEADS = 8
FEAT = 64

PAIR_IN, LEFT, RIGHT, VALUES, GRADS, LOGITS, PAIR_OUT, GW, WEIGHTS, GW_SUM, AVG, GW_ALL, GL = range(13)
PHASES = 13


def iota(shape, dim):
    return lax.broadcasted_iota(I32, shape, dim)


def matmul(a, b):
    return jnp.dot(a, b, preferred_element_type=F32)


def matmul_nt(a, b):
    return lax.dot_general(a, b, (((1,), (1,)), ((), ())), preferred_element_type=F32)


def matmul_tn(a, b):
    return lax.dot_general(a, b, (((0,), (0,)), ((), ())), preferred_element_type=F32)


def split(a):
    high = a.astype(BF16)
    return high, (a - high.astype(F32)).astype(BF16)


def normalize(a):
    center = a - jnp.mean(a, axis=-1, keepdims=True)
    inverse = lax.rsqrt(jnp.mean(center * center, axis=-1, keepdims=True) + EPS)
    return center * inverse, inverse


def swap_blocks(arrays, width):
    arrays = list(arrays)
    lanes = arrays[0].shape[1]
    block = iota(arrays[0].shape, 1) // width
    bit = len(arrays) // 2
    while bit:
        upper = (block & bit) != 0
        for low in range(len(arrays)):
            if low & bit:
                continue
            a, b = arrays[low], arrays[low | bit]
            arrays[low] = jnp.where(upper, pltpu.roll(b, bit * width, 1), a)
            arrays[low | bit] = jnp.where(upper, b, pltpu.roll(a, lanes - bit * width, 1))
        bit //= 2
    return arrays


def kernel(
    mask_s, mask_v, x_ref, adj_ref, w1_ref, w2_ref, wc_ref, ws_ref, wf_ref, score_ref, m_hbm, pair_hbm,
    out_al, out_pair, out_grad,
    xn_scr, lbuf, rbuf, l_all, r_all, vbuf, gbuf, vh, gh, gate_scr, wf_blk, m_scr, m_hl,
    pin_tile, pin_scr, o_scr, p_scr, po_scr, po_tile, po_all, lg_src, lg_all, prob_scr, wbuf, wh,
    avbuf, avrx, gwbuf, gwrx, rsbuf, rsrx, agbuf, agrx, glbuf, glrx, gl_scr,
    send_sem, recv_sem, local_sem,
):
    S = lax.axis_index("seq")
    row = lax.axis_index("row")
    col = lax.axis_index("col")
    T = row * NC + col
    y = S // NC
    xpos = S % NC

    def device(s, t):
        return (s, t // NC, t % NC)

    def remote(src, dst, phase, s, t):
        return pltpu.make_async_remote_copy(
            src_ref=src, dst_ref=dst, send_sem=send_sem.at[phase], recv_sem=recv_sem.at[phase],
            device_id=device(s, t), device_id_type=MESH,
        )

    def local(src, dst, phase):
        pltpu.make_async_copy(src, dst, recv_sem.at[phase]).start()

    def wait_recv(buf, phase):
        pltpu.make_async_copy(buf, buf, recv_sem.at[phase]).wait()

    def wait_send(buf, phase):
        pltpu.make_async_copy(buf, buf, send_sem.at[phase]).wait()

    barrier = pltpu.get_barrier_semaphore()

    def greet(s, t):
        pl.semaphore_signal(barrier, inc=1, device_id=device(s, t), device_id_type=MESH)

    @pl.loop(1, N)
    def _(d):
        greet((S + d) % N, T)
        greet(S, (T + d) % N)
        greet((S + d) % N, S)

    @pl.when(S != T)
    def _():
        greet(S, S)

    @pl.loop(0, N)
    def _(e):
        s, t = col * NC + e // NC, row * NC + e % NC

        @pl.when(jnp.logical_or(s != S, t != T))
        def _():
            greet(s, t)

    m_copy = pltpu.make_async_copy(m_hbm, m_scr, local_sem.at[0])
    m_copy.start()

    xn = normalize(x_ref[...].reshape(SEQ * TOK, FEAT).astype(F32))[0].astype(BF16).astype(F32)
    xn_scr[...] = xn

    lane = iota((32, 256), 1)
    chan = iota((32, 256), 0)
    same = lane % 32 == chan
    pick_left = jnp.where(jnp.logical_and(same, lane < 128), 1.0, 0.0).astype(BF16)
    pick_right = jnp.where(jnp.logical_and(same, lane >= 128), 1.0, 0.0).astype(BF16)
    both = matmul(w1_ref[...], pick_left) + matmul(w2_ref[...], pick_right)
    quarter = (iota((FEAT, 256), 1) // 32) % 4
    w_lr = jnp.concatenate([jnp.where(quarter == q, both, 0.0) for q in range(4)], axis=0).astype(BF16)
    x_lr = []
    for q in range(4):
        parts = []
        for group in range(4):
            token = 4 * group + q
            parts.append(
                xn_scr[pl.ds(token, SEQ, stride=TOK), :] * mask_s[T * TOK + token].astype(F32)
            )
        x_lr.append(jnp.concatenate(parts, axis=0))
    factors = matmul(jnp.concatenate(x_lr, axis=1).astype(BF16), w_lr).astype(BF16)
    lbuf[...] = factors[:, :128].reshape(4, SEQ, 128)
    rbuf[...] = factors[:, 128:].reshape(4, SEQ, 128)

    pl.semaphore_wait(
        barrier,
        4 * N - 2 - jnp.where(S == T, 1, 0).astype(I32) - jnp.where(y == col, 1, 0).astype(I32),
    )

    my_tile = pair_hbm.at[pl.ds(col * TOK, TOK), pl.ds(xpos * TOK, TOK), :]

    @pl.when(y == col)
    def _():
        local(my_tile, pin_tile, PAIR_IN)

        @pl.loop(1, NC)
        def _(d):
            c = (col + d) % NC
            remote(
                pair_hbm.at[pl.ds(c * TOK, TOK), pl.ds(xpos * TOK, TOK), :], pin_tile, PAIR_IN, S, row * NC + c
            ).start()

    mine = pl.ds(S * SEQ, SEQ)
    local(lbuf, l_all.at[:, mine, :], LEFT)

    @pl.when(S == T)
    def _():
        local(rbuf, r_all.at[:, mine, :], RIGHT)

    @pl.when(S != T)
    def _():
        remote(rbuf, r_all.at[:, mine, :], RIGHT, T, T).start()

    @pl.loop(1, N)
    def _(d):
        remote(lbuf, l_all.at[:, mine, :], LEFT, (S + d) % N, T).start()
        remote(rbuf, r_all.at[:, mine, :], RIGHT, T, (T + d) % N).start()

    lane = iota((256, 1024), 1)
    chan = iota((256, 1024), 0)
    pick = jnp.where(
        jnp.logical_and(lane // 128 == chan // 32, lane % 32 == chan % 32), 1.0, 0.0
    ).astype(BF16)
    quarter = (iota((FEAT, 1024), 1) // 32) % 4

    def spread(w):
        return jnp.concatenate([jnp.where(quarter == q, w, 0.0) for q in range(4)], axis=0).astype(BF16)

    def by_group(a):
        a = a.reshape(8, 4, TOK, FEAT)
        return jnp.concatenate([a[:, q].reshape(8 * TOK, FEAT) for q in range(4)], axis=1)

    def to_pieces(a, buf):
        for h in range(HEADS):
            buf[2 * h : 2 * h + 2] = a[:, h * 128 : (h + 1) * 128].reshape(2, 4, TOK, 128)

    tokens = pl.ds(T * TOK, TOK)

    def send_column(buf, dst, phase):
        local(buf.at[T], dst, phase)

        @pl.loop(1, N)
        def _(d):
            t = (T + d) % N
            remote(buf.at[t], dst, phase, S, t).start()

    x_v = by_group(xn).astype(BF16)
    to_pieces(matmul(x_v, spread(matmul(wc_ref[...], pick))).astype(BF16), vbuf)
    send_column(vbuf, vh.at[:, tokens, :], VALUES)
    gate = jax.nn.sigmoid(matmul(x_v, spread(matmul(ws_ref[...], pick))))
    gate_scr[...] = gate
    wf_blk[...] = spread(matmul_tn(wf_ref[...], pick))
    x_g = by_group(adj_ref[...].astype(F32)).astype(BF16)
    to_pieces((matmul(x_g, wf_blk[...]) * gate).astype(BF16), gbuf)
    send_column(gbuf, gh.at[:, tokens, :], GRADS)

    m_copy.wait()
    m_high, m_low = split(m_scr[...])
    m_hl[:, :128] = m_high
    m_hl[:, 128:] = m_low
    score = score_ref[...]
    repeat = jnp.where(iota((HEADS, 128), 1) // TOK == iota((HEADS, 128), 0), 1.0, 0.0).astype(BF16)

    def repeated(a):
        high, low = split(a)
        return matmul(high, repeat).astype(BF16), matmul(low, repeat).astype(BF16)

    score_high, score_low = repeated(score)
    wait_recv(pin_tile, PAIR_IN)
    pin_scr[...] = pin_tile[...].reshape(TOK * TOK, 128).astype(F32)

    wait_recv(l_all, LEFT)
    wait_recv(r_all, RIGHT)
    left = jnp.concatenate([l_all[g] for g in range(4)], axis=1)
    right = jnp.concatenate([r_all[g] for g in range(4)], axis=1)
    outer = matmul_tn(left, right)
    for g in range(4):
        o_scr[g] = outer[:, g * 128 : (g + 1) * 128]

    @pl.loop(0, 8)
    def _(cg):
        parts = [
            jnp.concatenate([o_scr[g, pl.ds(4 * cg + q, TOK, stride=32), :] for g in range(4)], axis=0)
            for q in range(4)
        ]
        parts = swap_blocks(parts, 32)
        lanes = pl.ds(pl.multiple_of(cg * 128, 128), 128)
        for j in range(TOK):
            p_scr[pl.ds(j * TOK, TOK), lanes] = parts[j % 4][(j // 4) * TOK : (j // 4 + 1) * TOK]

    p_high, p_low = split(p_scr[...])
    product = matmul(p_high, m_hl[...])
    update = product[:, :128] + (product[:, 128:] + matmul(p_low, m_hl[:, :128]))
    pin = jnp.concatenate([pin_scr[pl.ds(j, TOK, stride=TOK), :] for j in range(TOK)], axis=0)
    pair_tile = (pin + update).astype(BF16).astype(F32)
    normal = normalize(pair_tile)[0]
    n_high, n_low = split(normal)
    logits = matmul(n_high, score_high) + (matmul(n_high, score_low) + matmul(n_low, score_high))
    own = iota((TOK, 1, 128), 2) % TOK == iota((TOK, 1, 128), 0)
    lg_src[...] = jnp.sum(jnp.where(own, logits.reshape(TOK, TOK, 128), 0.0), axis=0)

    def send_plane(src, dst, phase):
        local(src, dst, phase)

        @pl.loop(1, N)
        def _(d):
            remote(src, dst, phase, (S + d) % N, T).start()

    send_plane(lg_src, lg_all.at[S], LOGITS)
    po_scr[...] = pair_tile
    for i in range(TOK):
        po_tile[i] = po_scr[pl.ds(i, TOK, stride=TOK), :].astype(BF16)
    place = po_all.at[pl.ds(col * TOK, TOK), pl.ds(xpos * TOK, TOK), :]
    owner = row * NC + y

    @pl.when(y == col)
    def _():
        local(po_tile, place, PAIR_OUT)

    @pl.when(y != col)
    def _():
        remote(po_tile, place, PAIR_OUT, S, owner).start()

    @pl.loop(1, N)
    def _(d):
        remote(po_tile, place, PAIR_OUT, (S + d) % N, owner).start()

    wait_recv(vh, VALUES)
    wait_recv(gh, GRADS)
    v_cat = jnp.concatenate([vh[g] for g in range(4)], axis=1)
    g_cat = jnp.concatenate([gh[g] for g in range(4)], axis=1)
    gwbuf[...] = matmul_nt(g_cat, v_cat).astype(BF16).reshape(N, TOK, 256)
    send_column(gwbuf, gwrx.at[T], GW)

    wait_recv(lg_all, LOGITS)
    lg = lg_all[...].reshape(2, 8, TOK, 128)
    parts = swap_blocks([lg[:, s].reshape(2 * TOK, 128) for s in range(8)], TOK)
    lg = jnp.stack([jnp.concatenate([a[:TOK], a[TOK:]], axis=1) for a in parts], axis=0)
    maskf = mask_v[...].astype(F32).reshape(1, 1, 256)
    lg = jnp.where(maskf > 0, lg, LOW)
    scaled = jnp.exp(lg - jnp.max(lg, axis=-1, keepdims=True)) * maskf
    prob = scaled / jnp.sum(scaled, axis=-1, keepdims=True)
    prob_scr[...] = prob
    wbuf[...] = prob.astype(BF16)
    local(wbuf.at[T // 2], wh.at[tokens, :], WEIGHTS)

    @pl.loop(1, N)
    def _(d):
        t = (T + d) % N
        remote(wbuf.at[t // 2], wh.at[tokens, :], WEIGHTS, S, t).start()

    wait_recv(gwrx, GW)
    gw = gwrx[...].astype(F32).reshape(HEADS, 2, TOK, 256)
    gw = (gw[:, 0] + gw[:, 1]).astype(BF16)
    for h in range(HEADS):
        rsbuf[2 * h] = gw[h, :, :128]
        rsbuf[2 * h + 1] = gw[h, :, 128:]
    local(rsbuf.at[S], rsrx.at[S], GW_SUM)

    @pl.loop(1, N)
    def _(d):
        s = (S + d) % N
        remote(rsbuf.at[s], rsrx.at[S], GW_SUM, s, T).start()

    wait_recv(wh, WEIGHTS)
    avg = matmul(wh[...], v_cat).astype(BF16)
    for g in range(4):
        avbuf[:, g] = avg[:, g * 128 : (g + 1) * 128].reshape(N, TOK, 128)
    send_column(avbuf, avrx.at[T], AVG)

    wait_recv(rsrx, GW_SUM)
    agbuf[...] = jnp.sum(rsrx[...].astype(F32), axis=0).astype(BF16)
    send_plane(agbuf, agrx.at[S], GW_ALL)

    wait_recv(agrx, GW_ALL)
    gw = agrx[...].astype(F32).reshape(HEADS, 2, TOK, 128)
    gw = jnp.concatenate([gw[:, 0], gw[:, 1]], axis=-1)
    prob = prob_scr[...]
    gl = prob * (gw - jnp.sum(prob * gw, axis=-1, keepdims=True))
    parts = [jnp.concatenate([gl[h, :, :128], gl[h, :, 128:]], axis=0) for h in range(HEADS)]
    parts = swap_blocks(parts, TOK)
    for s in range(8):
        glbuf[s // 4, s % 4] = parts[s][:TOK].astype(BF16)
        glbuf[2 + s // 4, s % 4] = parts[s][TOK:].astype(BF16)
    local(glbuf.at[col], glrx.at[col], GL)

    @pl.loop(1, NC)
    def _(d):
        c = (col + d) % NC
        remote(glbuf.at[c], glrx.at[col], GL, S, row * NC + c).start()

    wait_recv(avrx, AVG)
    gated = jnp.concatenate(
        [avrx[2 * h : 2 * h + 2].reshape(8 * TOK, 128).astype(F32) for h in range(HEADS)], axis=1
    )
    gated = (gated * gate_scr[...]).astype(BF16)
    mixed = matmul_nt(gated, wf_blk[...])
    result = (by_group(x_ref[...].astype(F32)) + mixed).astype(BF16)
    for q in range(4):
        out_al[:, q] = result[:, q * FEAT : (q + 1) * FEAT].reshape(8, TOK, FEAT)

    wait_recv(po_all, PAIR_OUT)
    po_copy = pltpu.make_async_copy(po_all, out_pair, local_sem.at[1])
    po_copy.start()
    center = score - jnp.mean(score, axis=0, keepdims=True)
    c_high, c_low = repeated(center)
    c_hl = jnp.concatenate([c_high, c_low], axis=0)
    own = (iota((1, 1, TOK, 128), 3) % TOK) == iota((1, 1, TOK, 128), 2)
    wait_recv(glrx, GL)
    for c in range(NC):
        for s in range(NC):
            gl_scr[pl.ds(c * TOK, TOK), s] = glrx[c, s].astype(F32).reshape(TOK, 1, 128)
    rows_at_once = 8

    @pl.loop(0, 64 // rows_at_once)
    def _(b):
        rows = pl.ds(b * rows_at_once, rows_at_once)
        block = po_all[rows].reshape(rows_at_once * 64, 128).astype(F32)
        normal, inverse = normalize(block)
        spread_gl = jnp.where(own, gl_scr[rows], 0.0)
        spread_gl = spread_gl.astype(BF16).reshape(rows_at_once * 64, 128)
        grad = matmul_nt(spread_gl, c_hl)
        grad = grad[:, :128] + grad[:, 128:]
        along = jnp.mean(grad * normal, axis=-1, keepdims=True)
        out_grad[rows] = (inverse * (grad - normal * along)).astype(BF16).reshape(rows_at_once, 64, 128)

    po_copy.wait()

    @pl.when(y == col)
    def _():
        third = pair_hbm.at[pl.ds(0, 3 * TOK), pl.ds(0, TOK), :]
        wait_send(third, PAIR_IN)
        wait_send(po_all.at[pl.ds(0, 60)], PAIR_OUT)

    @pl.when(y != col)
    def _():
        wait_send(po_all, PAIR_OUT)

    wait_send(l_all.at[:, pl.ds(0, 15 * SEQ), :], LEFT)

    @pl.when(S == T)
    def _():
        wait_send(r_all.at[:, pl.ds(0, 15 * SEQ), :], RIGHT)

    @pl.when(S != T)
    def _():
        wait_send(r_all, RIGHT)

    wait_send(vh.at[:, pl.ds(0, 15 * TOK), :], VALUES)
    wait_send(gh.at[:, pl.ds(0, 15 * TOK), :], GRADS)
    wait_send(lg_all.at[pl.ds(0, 15)], LOGITS)
    wait_send(gwrx.at[pl.ds(0, 15)], GW)
    wait_send(wh.at[pl.ds(0, 15 * TOK), :], WEIGHTS)
    wait_send(rsrx.at[pl.ds(0, 15)], GW_SUM)
    wait_send(avrx.at[pl.ds(0, 15)], AVG)
    wait_send(agrx.at[pl.ds(0, 15)], GW_ALL)
    wait_send(glrx.at[pl.ds(0, 3)], GL)


def on_device(
    alignment_input,
    pair_input,
    token_valid_mask,
    first_factor_weights,
    second_factor_weights,
    content_weights_grid,
    sigmoid_weights_grid,
    outer_matrix,
    score_matrix,
    final_mixing_weights,
    adjoint_of_rowset,
):
    vmem = pl.BlockSpec(memory_space=pltpu.VMEM)
    smem = pl.BlockSpec(memory_space=pltpu.SMEM)
    anywhere = pl.BlockSpec(memory_space=pl.ANY)
    V = pltpu.VMEM
    scratch = [
        V((SEQ * TOK, FEAT), F32),
        V((4, SEQ, 128), BF16),
        V((4, SEQ, 128), BF16),
        V((4, N * SEQ, 128), BF16),
        V((4, N * SEQ, 128), BF16),
        V((N, 4, TOK, 128), BF16),
        V((N, 4, TOK, 128), BF16),
        V((4, 256, 128), BF16),
        V((4, 256, 128), BF16),
        V((128, 1024), F32),
        V((256, 1024), BF16),
        V((1024, 128), F32),
        V((1024, 256), BF16),
        V((TOK, TOK, 128), BF16),
        V((TOK * TOK, 128), F32),
        V((4, 512, 128), F32),
        V((256, 1024), F32),
        V((256, 128), F32),
        V((TOK, TOK, 128), BF16),
        V((64, 64, 128), BF16),
        V((TOK, 128), F32),
        V((N, TOK, 128), F32),
        V((HEADS, TOK, 256), F32),
        V((HEADS, TOK, 256), BF16),
        V((256, 256), BF16),
        V((N, 4, TOK, 128), BF16),
        V((N, 4, TOK, 128), BF16),
        V((N, TOK, 256), BF16),
        V((N, TOK, 256), BF16),
        V((N, TOK, 128), BF16),
        V((N, TOK, 128), BF16),
        V((TOK, 128), BF16),
        V((N, TOK, 128), BF16),
        V((NC, NC, TOK, 128), BF16),
        V((NC, NC, TOK, 128), BF16),
        V((64, NC, 1, 128), F32),
        pltpu.SemaphoreType.DMA((PHASES,)),
        pltpu.SemaphoreType.DMA((PHASES,)),
        pltpu.SemaphoreType.DMA((2,)),
    ]
    grouped = (8, 4, TOK, FEAT)
    aligned, pair_output, pair_gradient = pl.pallas_call(
        kernel,
        out_shape=[
            jax.ShapeDtypeStruct(grouped, BF16),
            jax.ShapeDtypeStruct((64, 64, 128), BF16),
            jax.ShapeDtypeStruct((64, 64, 128), BF16),
        ],
        in_specs=[smem] + [vmem] * 9 + [anywhere] * 2,
        out_specs=[vmem, anywhere, vmem],
        scratch_shapes=scratch,
        compiler_params=pltpu.CompilerParams(
            collective_id=0, has_side_effects=True, vmem_limit_bytes=48 * 1024 * 1024
        ),
        name="msa_block",
    )(
        token_valid_mask,
        token_valid_mask.reshape(1, 256),
        alignment_input.reshape(grouped),
        adjoint_of_rowset.reshape(grouped),
        first_factor_weights,
        second_factor_weights,
        content_weights_grid,
        sigmoid_weights_grid,
        final_mixing_weights,
        score_matrix,
        outer_matrix,
        pair_input,
    )
    return aligned.reshape(SEQ, TOK, FEAT), pair_output, pair_gradient


def solution(mesh):
    in_specs = (
        P("seq", ("row", "col"), None),
        P("row", "col", None),
        P(),
        P(),
        P(),
        P(),
        P(),
        P(),
        P(),
        P(),
        P("seq", ("row", "col"), None),
    )
    out_specs = (P("seq", ("row", "col"), None), P("row", "col", None), P("row", "col", None))
    return jax.shard_map(
        on_device, mesh=mesh, in_specs=in_specs, out_specs=out_specs, check_vma=False
    )
```

```python
import jax
import jax.numpy as jnp
from jax import lax
from jax.experimental import pallas as pl
from jax.experimental.pallas import tpu as pltpu
from jax.sharding import PartitionSpec as P

F32 = jnp.float32
BF16 = jnp.bfloat16
I32 = jnp.int32
EPS = 1e-05
LOW = -1e30
MESH = pl.DeviceIdType.MESH

N = 16
NC = 4
TOK = 16
SEQ = 32
HEADS = 8
FEAT = 64

PAIR_IN, LEFT, SWAP, RIGHT, RIGHT_SIB, NORM, NORM_SIB, LOGITS, TURN, PAIR_OUT, GW_SUM, GW_ALL, GL = range(13)
PHASES = 13


def iota(shape, dim):
    return lax.broadcasted_iota(I32, shape, dim)


def matmul(a, b):
    return jnp.dot(a, b, preferred_element_type=F32)


def matmul_nt(a, b):
    return lax.dot_general(a, b, (((1,), (1,)), ((), ())), preferred_element_type=F32)


def matmul_tn(a, b):
    return lax.dot_general(a, b, (((0,), (0,)), ((), ())), preferred_element_type=F32)


def split(a):
    high = a.astype(BF16)
    return high, (a - high.astype(F32)).astype(BF16)


def normalize(a):
    center = a - jnp.mean(a, axis=-1, keepdims=True)
    inverse = lax.rsqrt(jnp.mean(center * center, axis=-1, keepdims=True) + EPS)
    return center * inverse, inverse


def swap_blocks(arrays, width):
    arrays = list(arrays)
    lanes = arrays[0].shape[1]
    block = iota(arrays[0].shape, 1) // width
    bit = len(arrays) // 2
    while bit:
        upper = (block & bit) != 0
        for low in range(len(arrays)):
            if low & bit:
                continue
            a, b = arrays[low], arrays[low | bit]
            arrays[low] = jnp.where(upper, pltpu.roll(b, bit * width, 1), a)
            arrays[low | bit] = jnp.where(upper, b, pltpu.roll(a, lanes - bit * width, 1))
        bit //= 2
    return arrays


def kernel(
    mask_s, x_hbm, adj_hbm, w1_hbm, w2_hbm, wc_hbm, ws_hbm, wf_hbm, score_hbm, m_hbm, pair_hbm,
    out_al, out_pair, out_grad,
    x_ref, adj_ref, w1_ref, w2_ref, wc_ref, ws_ref, wf_ref, score_ref, m_scr,
    xn_scr, lbuf, rbuf, rmid, l_all, r_all, nbuf, nv, vh, gbuf, gate_scr, wc_blk, wf_blk, m_hl,
    pin_tile, pin_scr, o_scr, p_scr, po_scr, po_tile, po_mid, po_all, lg_src, lg_all, prob_scr,
    rsbuf, rsrx, agbuf, agrx, glbuf, glrx, gl_scr,
    send_sem, recv_sem, local_sem,
):
    S = lax.axis_index("seq")
    row = lax.axis_index("row")
    col = lax.axis_index("col")
    T = row * NC + col
    y = S // NC
    xpos = S % NC
    core = T % 2
    sibling = T + 1 - 2 * core

    def slot(n):
        return (n % 2) * (N // 2) + n // 2

    def device(s, t):
        return (s, t // NC, t % NC)

    def remote(src, dst, phase, s, t):
        return pltpu.make_async_remote_copy(
            src_ref=src, dst_ref=dst, send_sem=send_sem.at[phase], recv_sem=recv_sem.at[phase],
            device_id=device(s, t), device_id_type=MESH,
        )

    def local(src, dst, phase):
        pltpu.make_async_copy(src, dst, recv_sem.at[phase]).start()

    def wait_recv(buf, phase):
        pltpu.make_async_copy(buf, buf, recv_sem.at[phase]).wait()

    def wait_send(buf, phase):
        pltpu.make_async_copy(buf, buf, send_sem.at[phase]).wait()

    loads = []
    for n, (src, dst) in enumerate(
        [
            (x_hbm, x_ref), (w1_hbm, w1_ref), (w2_hbm, w2_ref), (wc_hbm, wc_ref), (ws_hbm, ws_ref),
            (wf_hbm, wf_ref), (adj_hbm, adj_ref), (score_hbm, score_ref), (m_hbm, m_scr),
        ]
    ):
        copy = pltpu.make_async_copy(src, dst, local_sem.at[n])
        copy.start()
        loads.append(copy)

    barrier = pltpu.get_barrier_semaphore()

    def greet(s, t):
        pl.semaphore_signal(barrier, inc=1, device_id=device(s, t), device_id_type=MESH)

    @pl.loop(1, N)
    def _(d):
        greet((S + d) % N, T)

    @pl.loop(1, N // 2)
    def _(d):
        greet(S, (T + 2 * d) % N)

    greet(S, sibling)

    @pl.loop(1, NC)
    def _(d):
        greet(S, row * NC + (col + d) % NC)

    @pl.when(S != T)
    def _():
        greet(T, S)

    @pl.when(y != col)
    def _():
        greet(col * NC + xpos, row * NC + y)

    greeted = N - 1 + N // 2 - 1 + 1 + NC - 1
    greeted = greeted + jnp.where(S != T, 1, 0).astype(I32) + jnp.where(y != col, 1, 0).astype(I32)

    loads[0].wait()
    xn = normalize(x_ref[...].reshape(SEQ * TOK, FEAT).astype(F32))[0].astype(BF16).astype(F32)
    xn_scr[...] = xn

    def by_group(a):
        a = a.reshape(8, 4, TOK, FEAT)
        return jnp.concatenate([a[:, q].reshape(8 * TOK, FEAT) for q in range(4)], axis=1)

    x_v = by_group(xn).astype(BF16)
    nbuf[...] = x_v.reshape(8, TOK, 256)

    loads[1].wait()
    loads[2].wait()
    lane = iota((32, 256), 1)
    chan = iota((32, 256), 0)
    same = lane % 32 == chan
    pick_left = jnp.where(jnp.logical_and(same, lane < 128), 1.0, 0.0).astype(BF16)
    pick_right = jnp.where(jnp.logical_and(same, lane >= 128), 1.0, 0.0).astype(BF16)
    both = matmul_tn(w1_ref[...], pick_left) + matmul_tn(w2_ref[...], pick_right)
    quarter = (iota((FEAT, 256), 1) // 32) % 4
    w_lr = jnp.concatenate([jnp.where(quarter == q, both, 0.0) for q in range(4)], axis=0).astype(BF16)
    x_lr = []
    for q in range(4):
        parts = []
        for group in range(4):
            token = 4 * group + q
            parts.append(
                xn_scr[pl.ds(token, SEQ, stride=TOK), :] * mask_s[T * TOK + token].astype(F32)
            )
        x_lr.append(jnp.concatenate(parts, axis=0))
    factors = matmul(jnp.concatenate(x_lr, axis=1).astype(BF16), w_lr).astype(BF16)
    lbuf[...] = factors[:, :128].reshape(4, SEQ, 128)
    rbuf[...] = factors[:, 128:].reshape(4, SEQ, 128)

    pl.semaphore_wait(barrier, greeted)

    @pl.when(S == T)
    def _():
        local(rbuf, rmid, SWAP)

    @pl.when(S != T)
    def _():
        remote(rbuf, rmid, SWAP, T, S).start()

    mine = pl.ds(slot(S) * SEQ, SEQ)
    local(lbuf, l_all.at[:, mine, :], LEFT)

    @pl.loop(1, N)
    def _(d):
        remote(lbuf, l_all.at[:, mine, :], LEFT, (S + d) % N, T).start()

    tokens = pl.ds(slot(T) * TOK, TOK)

    def send_norm(d):
        remote(nbuf, nv.at[:, tokens, :], NORM, S, (T + 2 * d) % N).start()

    local(nbuf, nv.at[:, tokens, :], NORM)
    for d in (1, 7, 2, 6):
        send_norm(d)

    my_tile = pair_hbm.at[pl.ds(col * TOK, TOK), pl.ds(xpos * TOK, TOK), :]

    @pl.when(y == col)
    def _():
        local(my_tile, pin_tile, PAIR_IN)

        @pl.loop(1, NC)
        def _(d):
            c = (col + d) % NC
            remote(
                pair_hbm.at[pl.ds(c * TOK, TOK), pl.ds(xpos * TOK, TOK), :], pin_tile, PAIR_IN, S, row * NC + c
            ).start()

    lane = iota((256, 1024), 1)
    chan = iota((256, 1024), 0)
    pick = jnp.where(
        jnp.logical_and(lane // 128 == chan // 32, lane % 32 == chan % 32), 1.0, 0.0
    ).astype(BF16)
    quarter = (iota((FEAT, 1024), 1) // 32) % 4

    def spread(w):
        return jnp.concatenate([jnp.where(quarter == q, w, 0.0) for q in range(4)], axis=0).astype(BF16)

    loads[3].wait()
    wc_blk[...] = spread(matmul(wc_ref[...], pick))

    wait_recv(rmid, SWAP)
    piece = pl.ds(slot(T) * SEQ, SEQ)
    local(rmid, r_all.at[:, piece, :], RIGHT)

    @pl.loop(1, N // 2)
    def _(d):
        remote(rmid, r_all.at[:, piece, :], RIGHT, S, (T + 2 * d) % N).start()

    for d in (3, 5, 4):
        send_norm(d)

    loads[4].wait()
    gate = jax.nn.sigmoid(matmul(x_v, spread(matmul(ws_ref[...], pick))))
    gate_scr[...] = gate
    loads[5].wait()
    wf_blk[...] = spread(matmul(wf_ref[...], pick))
    loads[6].wait()
    x_g = by_group(adj_ref[...].astype(F32)).astype(BF16)
    gbuf[...] = (matmul(x_g, wf_blk[...]) * gate).astype(BF16)

    loads[7].wait()
    loads[8].wait()
    m_high, m_low = split(m_scr[...])
    m_hl[:, :128] = m_high
    m_hl[:, 128:] = m_low
    score = score_ref[...]
    repeat = jnp.where(iota((HEADS, 128), 1) // TOK == iota((HEADS, 128), 0), 1.0, 0.0).astype(BF16)

    def repeated(a):
        high, low = split(a)
        return matmul_tn(high, repeat).astype(BF16), matmul_tn(low, repeat).astype(BF16)

    score_high, score_low = repeated(score)
    lane = iota((1, 128), 1) % TOK
    valid = jnp.zeros((1, 128), F32)
    for j in range(TOK):
        valid = jnp.where(lane == j, mask_s[S * TOK + j].astype(F32), valid)
    wait_recv(pin_tile, PAIR_IN)
    pin_scr[...] = pin_tile[...].reshape(TOK * TOK, 128).astype(F32)
    pin = jnp.concatenate([pin_scr[pl.ds(j, TOK, stride=TOK), :] for j in range(TOK)], axis=0)

    half = pl.ds(core * (N // 2) * SEQ, (N // 2) * SEQ)
    wait_recv(r_all.at[:, half, :], RIGHT)
    remote(r_all.at[:, half, :], r_all.at[:, half, :], RIGHT_SIB, S, sibling).start()

    wait_recv(l_all, LEFT)
    wait_recv(r_all.at[:, pl.ds((1 - core) * (N // 2) * SEQ, (N // 2) * SEQ), :], RIGHT_SIB)
    left = jnp.concatenate([l_all[g] for g in range(4)], axis=1)
    right = jnp.concatenate([r_all[g] for g in range(4)], axis=1)
    outer = matmul_tn(left, right)
    for g in range(4):
        o_scr[g] = outer[:, g * 128 : (g + 1) * 128]

    @pl.loop(0, 8)
    def _(cg):
        parts = [
            jnp.concatenate([o_scr[g, pl.ds(4 * cg + q, TOK, stride=32), :] for g in range(4)], axis=0)
            for q in range(4)
        ]
        parts = swap_blocks(parts, 32)
        lanes = pl.ds(pl.multiple_of(cg * 128, 128), 128)
        for j in range(TOK):
            p_scr[pl.ds(j * TOK, TOK), lanes] = parts[j % 4][(j // 4) * TOK : (j // 4 + 1) * TOK]

    p_high, p_low = split(p_scr[...])
    product = matmul(p_high, m_hl[...])
    update = product[:, :128] + (product[:, 128:] + matmul(p_low, m_hl[:, :128]))
    pair_tile = (pin + update).astype(BF16).astype(F32)
    normal = normalize(pair_tile)[0]
    n_high, n_low = split(normal)
    logits = matmul(n_high, score_high) + (matmul(n_high, score_low) + matmul(n_low, score_high))
    own = iota((TOK, 1, 128), 2) % TOK == iota((TOK, 1, 128), 0)
    logits = jnp.sum(jnp.where(own, logits.reshape(TOK, TOK, 128), 0.0), axis=0)
    lg_src[...] = jnp.where(valid > 0, logits, LOW)

    def send_plane(src, dst, phase):
        local(src, dst, phase)

        @pl.loop(1, N)
        def _(d):
            remote(src, dst, phase, (S + d) % N, T).start()

    send_plane(lg_src, lg_all.at[slot(S)], LOGITS)

    po_scr[...] = pair_tile
    for i in range(TOK):
        po_tile[i] = po_scr[pl.ds(i, TOK, stride=TOK), :].astype(BF16)

    @pl.when(y == col)
    def _():
        local(po_tile, po_mid, TURN)

    @pl.when(y != col)
    def _():
        remote(po_tile, po_mid, TURN, col * NC + xpos, row * NC + y).start()

    half = pl.ds(core * (N // 2) * TOK, (N // 2) * TOK)
    wait_recv(nv.at[:, half, :], NORM)
    remote(nv.at[:, half, :], nv.at[:, half, :], NORM_SIB, S, sibling).start()

    wait_recv(po_mid, TURN)
    send_plane(po_mid, po_all.at[pl.ds(y * TOK, TOK), pl.ds(xpos * TOK, TOK), :], PAIR_OUT)

    wait_recv(nv.at[:, pl.ds((1 - core) * (N // 2) * TOK, (N // 2) * TOK), :], NORM_SIB)

    @pl.loop(0, 8)
    def _(g):
        vh[g] = matmul(nv[g], wc_blk[...]).astype(BF16)

    def head(ref, h):
        return [ref[g, :, h * 128 : (h + 1) * 128] for g in range(8)]

    for h in range(HEADS):
        gw = matmul_nt(
            jnp.concatenate([gbuf[g * TOK : (g + 1) * TOK, h * 128 : (h + 1) * 128] for g in range(8)], axis=1),
            jnp.concatenate(head(vh, h), axis=1),
        ).astype(BF16)
        rsbuf[2 * h] = gw[:, :128]
        rsbuf[2 * h + 1] = gw[:, 128:]
    local(rsbuf.at[S], rsrx.at[S], GW_SUM)

    @pl.loop(1, N)
    def _(d):
        s = (S + d) % N
        remote(rsbuf.at[s], rsrx.at[S], GW_SUM, s, T).start()

    wait_recv(lg_all, LOGITS)
    lg = lg_all[...].reshape(2, 8, TOK, 128)
    parts = swap_blocks([lg[:, s].reshape(2 * TOK, 128) for s in range(8)], TOK)
    lg = jnp.stack([jnp.concatenate([a[:TOK], a[TOK:]], axis=1) for a in parts], axis=0)
    scaled = jnp.exp(lg - jnp.max(lg, axis=-1, keepdims=True))
    prob = scaled / jnp.sum(scaled, axis=-1, keepdims=True)
    prob_scr[...] = prob

    wait_recv(rsrx, GW_SUM)
    agbuf[...] = jnp.sum(rsrx[...].astype(F32), axis=0).astype(BF16)
    send_plane(agbuf, agrx.at[S], GW_ALL)

    weights = prob_scr[...].astype(BF16)
    columns = []
    for h in range(HEADS):
        avg = matmul(weights[h], jnp.concatenate(head(vh, h), axis=1))
        avg = jnp.concatenate([avg[:, g * 128 : (g + 1) * 128] for g in range(8)], axis=0)
        columns.append((avg * gate_scr[:, h * 128 : (h + 1) * 128]).astype(BF16))
    mixed = matmul_nt(jnp.concatenate(columns, axis=1), wf_blk[...])
    result = (by_group(x_ref[...].astype(F32)) + mixed).astype(BF16)
    for q in range(4):
        out_al[:, q] = result[:, q * FEAT : (q + 1) * FEAT].reshape(8, TOK, FEAT)

    wait_recv(agrx, GW_ALL)
    gw = agrx[...].astype(F32).reshape(HEADS, 2, TOK, 128)
    gw = jnp.concatenate([gw[:, 0], gw[:, 1]], axis=-1)
    prob = prob_scr[...]
    gl = prob * (gw - jnp.sum(prob * gw, axis=-1, keepdims=True))
    parts = [jnp.concatenate([gl[h, :, :128], gl[h, :, 128:]], axis=0) for h in range(HEADS)]
    parts = swap_blocks(parts, TOK)
    for s in range(N):
        start = (s % 2) * TOK
        glbuf[s // NC, s % NC] = parts[s // 2][start : start + TOK].astype(BF16)
    local(glbuf.at[col], glrx.at[col], GL)

    @pl.loop(1, NC)
    def _(d):
        c = (col + d) % NC
        remote(glbuf.at[c], glrx.at[col], GL, S, row * NC + c).start()

    wait_recv(po_all, PAIR_OUT)
    po_copy = pltpu.make_async_copy(po_all, out_pair, local_sem.at[9])
    po_copy.start()
    center = score - jnp.mean(score, axis=1, keepdims=True)
    c_high, c_low = repeated(center)
    c_hl = jnp.concatenate([c_high, c_low], axis=0)
    own = (iota((1, 1, TOK, 128), 3) % TOK) == iota((1, 1, TOK, 128), 2)
    wait_recv(glrx, GL)
    for c in range(NC):
        for s in range(NC):
            gl_scr[pl.ds(c * TOK, TOK), s] = glrx[c, s].astype(F32).reshape(TOK, 1, 128)
    rows_at_once = 8

    @pl.loop(0, 64 // rows_at_once)
    def _(b):
        rows = pl.ds(b * rows_at_once, rows_at_once)
        block = po_all[rows].reshape(rows_at_once * 64, 128).astype(F32)
        normal, inverse = normalize(block)
        spread_gl = jnp.where(own, gl_scr[rows], 0.0)
        spread_gl = spread_gl.astype(BF16).reshape(rows_at_once * 64, 128)
        grad = matmul_nt(spread_gl, c_hl)
        grad = grad[:, :128] + grad[:, 128:]
        along = jnp.mean(grad * normal, axis=-1, keepdims=True)
        out_grad[rows] = (inverse * (grad - normal * along)).astype(BF16).reshape(rows_at_once, 64, 128)

    po_copy.wait()

    @pl.when(y == col)
    def _():
        wait_send(pair_hbm.at[pl.ds(0, 3 * TOK), pl.ds(0, TOK), :], PAIR_IN)

    @pl.when(y != col)
    def _():
        wait_send(po_tile, TURN)

    @pl.when(S != T)
    def _():
        wait_send(rbuf, SWAP)

    wait_send(l_all.at[:, pl.ds(0, 15 * SEQ), :], LEFT)
    wait_send(r_all.at[:, pl.ds(0, 7 * SEQ), :], RIGHT)
    wait_send(r_all.at[:, pl.ds(0, 8 * SEQ), :], RIGHT_SIB)
    wait_send(nv.at[:, pl.ds(0, 7 * TOK), :], NORM)
    wait_send(nv.at[:, pl.ds(0, 8 * TOK), :], NORM_SIB)
    wait_send(lg_all.at[pl.ds(0, 15)], LOGITS)
    wait_send(po_all.at[pl.ds(0, 60)], PAIR_OUT)
    wait_send(rsrx.at[pl.ds(0, 15)], GW_SUM)
    wait_send(agrx.at[pl.ds(0, 15)], GW_ALL)
    wait_send(glrx.at[pl.ds(0, 3)], GL)


def on_device(
    alignment_input,
    pair_input,
    token_valid_mask,
    first_factor_weights,
    second_factor_weights,
    content_weights_grid,
    sigmoid_weights_grid,
    outer_matrix,
    score_matrix,
    final_mixing_weights,
    adjoint_of_rowset,
):
    vmem = pl.BlockSpec(memory_space=pltpu.VMEM)
    smem = pl.BlockSpec(memory_space=pltpu.SMEM)
    hbm = pl.BlockSpec(memory_space=pltpu.HBM)
    V = pltpu.VMEM
    scratch = [
        V((8, 4, TOK, FEAT), BF16),
        V((8, 4, TOK, FEAT), BF16),
        V((32, FEAT), BF16),
        V((32, FEAT), BF16),
        V((FEAT, 256), BF16),
        V((FEAT, 256), BF16),
        V((FEAT, 256), BF16),
        V((HEADS, 128), F32),
        V((1024, 128), F32),
        V((SEQ * TOK, FEAT), F32),
        V((4, SEQ, 128), BF16),
        V((4, SEQ, 128), BF16),
        V((4, SEQ, 128), BF16),
        V((4, N * SEQ, 128), BF16),
        V((4, N * SEQ, 128), BF16),
        V((8, TOK, 256), BF16),
        V((8, 256, 256), BF16),
        V((8, 256, 1024), BF16),
        V((128, 1024), BF16),
        V((128, 1024), F32),
        V((256, 1024), BF16),
        V((256, 1024), BF16),
        V((1024, 256), BF16),
        V((TOK, TOK, 128), BF16),
        V((TOK * TOK, 128), F32),
        V((4, 512, 128), F32),
        V((256, 1024), F32),
        V((256, 128), F32),
        V((TOK, TOK, 128), BF16),
        V((TOK, TOK, 128), BF16),
        V((64, 64, 128), BF16),
        V((TOK, 128), F32),
        V((N, TOK, 128), F32),
        V((HEADS, TOK, 256), F32),
        V((N, TOK, 128), BF16),
        V((N, TOK, 128), BF16),
        V((TOK, 128), BF16),
        V((N, TOK, 128), BF16),
        V((NC, NC, TOK, 128), BF16),
        V((NC, NC, TOK, 128), BF16),
        V((64, NC, 1, 128), F32),
        pltpu.SemaphoreType.DMA((PHASES,)),
        pltpu.SemaphoreType.DMA((PHASES,)),
        pltpu.SemaphoreType.DMA((10,)),
    ]
    grouped = (8, 4, TOK, FEAT)
    aligned, pair_output, pair_gradient = pl.pallas_call(
        kernel,
        out_shape=[
            jax.ShapeDtypeStruct(grouped, BF16),
            jax.ShapeDtypeStruct((64, 64, 128), BF16),
            jax.ShapeDtypeStruct((64, 64, 128), BF16),
        ],
        in_specs=[smem] + [hbm] * 10,
        out_specs=[vmem, hbm, vmem],
        scratch_shapes=scratch,
        compiler_params=pltpu.CompilerParams(
            collective_id=0, has_side_effects=True, vmem_limit_bytes=60 * 1024 * 1024
        ),
        name="msa_block",
    )(
        token_valid_mask,
        alignment_input.reshape(grouped),
        adjoint_of_rowset.reshape(grouped),
        first_factor_weights.T,
        second_factor_weights.T,
        content_weights_grid,
        sigmoid_weights_grid,
        final_mixing_weights.T,
        score_matrix.T,
        outer_matrix,
        pair_input,
    )
    return aligned.reshape(SEQ, TOK, FEAT), pair_output, pair_gradient


def solution(mesh):
    in_specs = (
        P("seq", ("row", "col"), None),
        P("row", "col", None),
        P(),
        P(),
        P(),
        P(),
        P(),
        P(),
        P(),
        P(),
        P("seq", ("row", "col"), None),
    )
    out_specs = (P("seq", ("row", "col"), None), P("row", "col", None), P("row", "col", None))
    return jax.shard_map(
        on_device, mesh=mesh, in_specs=in_specs, out_specs=out_specs, check_vma=False
    )
```

```python
import jax
import jax.numpy as jnp
from jax import lax
from jax.experimental import pallas as pl
from jax.experimental.pallas import tpu as pltpu
from jax.sharding import PartitionSpec as P

F32 = jnp.float32
BF16 = jnp.bfloat16
I32 = jnp.int32
EPS = 1e-05
LOW = -1e30
MESH = pl.DeviceIdType.MESH

N = 16
NC = 4
TOK = 16
SEQ = 32
HEADS = 8
FEAT = 64

PAIR_IN, LEFT, RIGHT, RIGHT_SIB, NORM, NORM_SIB, LOGITS, TURN, A1, B1, A2, B2, GL_SUM, GL = range(14)
PHASES = 14


def iota(shape, dim):
    return lax.broadcasted_iota(I32, shape, dim)


def matmul(a, b):
    return jnp.dot(a, b, preferred_element_type=F32)


def matmul_nt(a, b):
    return lax.dot_general(a, b, (((1,), (1,)), ((), ())), preferred_element_type=F32)


def matmul_tn(a, b):
    return lax.dot_general(a, b, (((0,), (0,)), ((), ())), preferred_element_type=F32)


def split(a):
    high = a.astype(BF16)
    return high, (a - high.astype(F32)).astype(BF16)


def normalize(a):
    center = a - jnp.mean(a, axis=-1, keepdims=True)
    inverse = lax.rsqrt(jnp.mean(center * center, axis=-1, keepdims=True) + EPS)
    return center * inverse, inverse


def swap_blocks(arrays, width):
    arrays = list(arrays)
    lanes = arrays[0].shape[1]
    block = iota(arrays[0].shape, 1) // width
    bit = len(arrays) // 2
    while bit:
        upper = (block & bit) != 0
        for low in range(len(arrays)):
            if low & bit:
                continue
            a, b = arrays[low], arrays[low | bit]
            arrays[low] = jnp.where(upper, pltpu.roll(b, bit * width, 1), a)
            arrays[low | bit] = jnp.where(upper, b, pltpu.roll(a, lanes - bit * width, 1))
        bit //= 2
    return arrays


def kernel(
    mask_s, x_hbm, adj_hbm, w1_hbm, w2_hbm, wc_hbm, ws_hbm, wf_hbm, score_hbm, m_hbm, pair_hbm,
    out_al, out_pair, out_gl,
    x_ref, adj_ref, w1_ref, w2_ref, wc_ref, ws_ref, wf_ref, score_ref, m_scr,
    xn_scr, lbuf, rbuf, l_all, r_all, nbuf, nv, vh, gbuf, gate_scr, wc_blk, wf_blk, m_hl,
    pin_tile, pin_scr, o_scr, p_scr, po_scr, po_tile, po_mid, po_all, lg_src, lg_all, prob_scr,
    rsbuf, rsrx, gl_tile, gl_all,
    send_sem, recv_sem, local_sem,
):
    S = lax.axis_index("seq")
    row = lax.axis_index("row")
    col = lax.axis_index("col")
    T = row * NC + col
    y = S // NC
    xpos = S % NC
    core = T % 2
    sibling = T + 1 - 2 * core

    def slot(n):
        return (n % 2) * (N // 2) + n // 2

    def device(s, t):
        return (s, t // NC, t % NC)

    def remote(src, dst, phase, s, t):
        return pltpu.make_async_remote_copy(
            src_ref=src, dst_ref=dst, send_sem=send_sem.at[phase], recv_sem=recv_sem.at[phase],
            device_id=device(s, t), device_id_type=MESH,
        )

    def local(src, dst, phase):
        pltpu.make_async_copy(src, dst, recv_sem.at[phase]).start()

    def wait_recv(buf, phase):
        pltpu.make_async_copy(buf, buf, recv_sem.at[phase]).wait()

    def wait_send(buf, phase):
        pltpu.make_async_copy(buf, buf, send_sem.at[phase]).wait()

    loads = []
    for n, (src, dst) in enumerate(
        [
            (x_hbm, x_ref), (w1_hbm, w1_ref), (w2_hbm, w2_ref), (wc_hbm, wc_ref), (ws_hbm, ws_ref),
            (wf_hbm, wf_ref), (adj_hbm, adj_ref), (score_hbm, score_ref), (m_hbm, m_scr),
        ]
    ):
        copy = pltpu.make_async_copy(src, dst, local_sem.at[n])
        copy.start()
        loads.append(copy)

    barrier = pltpu.get_barrier_semaphore()

    def greet(s, t):
        pl.semaphore_signal(barrier, inc=1, device_id=device(s, t), device_id_type=MESH)

    for d in range(1, N):
        greet((S + d) % N, T)
    for d in range(1, N // 2):
        greet(S, (T + 2 * d) % N)
    greet(S, sibling)
    across = (sibling + 2) % 4
    greet(S, row * NC + across)

    def right_source(d):
        return (core + 2 * d + 2 * (S // 2)) % N

    for d in range(1, N // 2):
        greet(right_source(d), S)

    @pl.when(jnp.logical_or(right_source(0) != S, S != T))
    def _():
        greet(right_source(0), S)

    alone = jnp.logical_and(S == T, S % 2 == core)
    greeted = N - 1 + N // 2 - 1 + 2 + N // 2 - jnp.where(alone, 1, 0).astype(I32)

    loads[0].wait()
    xn = normalize(x_ref[...].reshape(SEQ * TOK, FEAT).astype(F32))[0].astype(BF16).astype(F32)
    xn_scr[...] = xn

    def by_group(a):
        a = a.reshape(8, 4, TOK, FEAT)
        return jnp.concatenate([a[:, q].reshape(8 * TOK, FEAT) for q in range(4)], axis=1)

    x_v = by_group(xn).astype(BF16)
    nbuf[...] = x_v.reshape(8, TOK, 256)

    loads[1].wait()
    loads[2].wait()
    lane = iota((32, 256), 1)
    chan = iota((32, 256), 0)
    same = lane % 32 == chan
    pick_left = jnp.where(jnp.logical_and(same, lane < 128), 1.0, 0.0).astype(BF16)
    pick_right = jnp.where(jnp.logical_and(same, lane >= 128), 1.0, 0.0).astype(BF16)
    both = matmul_tn(w1_ref[...], pick_left) + matmul_tn(w2_ref[...], pick_right)
    quarter = (iota((FEAT, 256), 1) // 32) % 4
    w_lr = jnp.concatenate([jnp.where(quarter == q, both, 0.0) for q in range(4)], axis=0).astype(BF16)
    x_lr = []
    for q in range(4):
        parts = []
        for group in range(4):
            token = 4 * group + q
            parts.append(
                xn_scr[pl.ds(token, SEQ, stride=TOK), :] * mask_s[T * TOK + token].astype(F32)
            )
        x_lr.append(jnp.concatenate(parts, axis=0))
    factors = matmul(jnp.concatenate(x_lr, axis=1).astype(BF16), w_lr).astype(BF16)
    lbuf[...] = factors[:, :128].reshape(4, SEQ, 128)
    rbuf[...] = factors[:, 128:].reshape(4, SEQ, 128)

    pl.semaphore_wait(barrier, greeted)

    parity = S % 2

    def send_right(d):
        remote(rbuf, r_all.at[slot(S)], RIGHT, T, (T - core + parity + 2 * d) % N).start()

    for d in (4, 3, 5, 2, 6, 1, 7):
        send_right(d)

    @pl.when(alone)
    def _():
        local(rbuf, r_all.at[slot(S)], RIGHT)

    @pl.when(jnp.logical_not(alone))
    def _():
        send_right(0)

    local(lbuf, l_all.at[slot(S)], LEFT)

    @pl.loop(1, N)
    def _(d):
        remote(lbuf, l_all.at[slot(S)], LEFT, (S + d) % N, T).start()

    my_tile = pair_hbm.at[pl.ds(col * TOK, TOK), pl.ds(xpos * TOK, TOK), :]

    @pl.when(y == col)
    def _():
        local(my_tile, pin_tile, PAIR_IN)

        @pl.loop(1, NC)
        def _(d):
            c = (col + d) % NC
            remote(
                pair_hbm.at[pl.ds(c * TOK, TOK), pl.ds(xpos * TOK, TOK), :], pin_tile, PAIR_IN, S, row * NC + c
            ).start()

    local(nbuf, nv.at[slot(T)], NORM)
    for d in (4, 3, 5, 2, 6, 1, 7):
        remote(nbuf, nv.at[slot(T)], NORM, S, (T + 2 * d) % N).start()

    lane = iota((256, 1024), 1)
    chan = iota((256, 1024), 0)
    pick = jnp.where(
        jnp.logical_and(lane // 128 == chan // 32, lane % 32 == chan % 32), 1.0, 0.0
    ).astype(BF16)
    quarter = (iota((FEAT, 1024), 1) // 32) % 4

    def spread(w):
        return jnp.concatenate([jnp.where(quarter == q, w, 0.0) for q in range(4)], axis=0).astype(BF16)

    loads[3].wait()
    wc_blk[...] = spread(matmul(wc_ref[...], pick))

    loads[4].wait()
    gate = jax.nn.sigmoid(matmul(x_v, spread(matmul(ws_ref[...], pick))))
    gate_scr[...] = gate
    loads[5].wait()
    wf_blk[...] = spread(matmul(wf_ref[...], pick))
    loads[6].wait()
    x_g = by_group(adj_ref[...].astype(F32)).astype(BF16)
    gbuf[...] = (matmul(x_g, wf_blk[...]) * gate).astype(BF16)

    loads[7].wait()
    loads[8].wait()
    m_high, m_low = split(m_scr[...])
    m_hl[:, :128] = m_high
    m_hl[:, 128:] = m_low
    score = score_ref[...]
    repeat = jnp.where(iota((HEADS, 128), 1) // TOK == iota((HEADS, 128), 0), 1.0, 0.0).astype(BF16)

    def repeated(a):
        high, low = split(a)
        return matmul_tn(high, repeat).astype(BF16), matmul_tn(low, repeat).astype(BF16)

    score_high, score_low = repeated(score)
    lane = iota((1, 128), 1) % TOK
    valid = jnp.zeros((1, 128), F32)
    for j in range(TOK):
        valid = jnp.where(lane == j, mask_s[S * TOK + j].astype(F32), valid)
    wait_recv(pin_tile, PAIR_IN)
    pin_scr[...] = pin_tile[...].reshape(TOK * TOK, 128).astype(F32)
    pin = jnp.concatenate([pin_scr[pl.ds(j, TOK, stride=TOK), :] for j in range(TOK)], axis=0)

    half = pl.ds(core * (N // 2), N // 2)
    other = pl.ds((1 - core) * (N // 2), N // 2)
    wait_recv(r_all.at[half], RIGHT)
    remote(r_all.at[half], r_all.at[half], RIGHT_SIB, S, sibling).start()

    wait_recv(l_all, LEFT)
    left = jnp.concatenate([l_all[:, g].reshape(N * SEQ, 128) for g in range(4)], axis=1)
    wait_recv(r_all.at[other], RIGHT_SIB)
    right = jnp.concatenate([r_all[:, g].reshape(N * SEQ, 128) for g in range(4)], axis=1)
    outer = matmul_tn(left, right)
    for g in range(4):
        o_scr[g] = outer[:, g * 128 : (g + 1) * 128]

    @pl.loop(0, 8)
    def _(cg):
        parts = [
            jnp.concatenate([o_scr[g, pl.ds(4 * cg + q, TOK, stride=32), :] for g in range(4)], axis=0)
            for q in range(4)
        ]
        parts = swap_blocks(parts, 32)
        lanes = pl.ds(pl.multiple_of(cg * 128, 128), 128)
        for j in range(TOK):
            p_scr[pl.ds(j * TOK, TOK), lanes] = parts[j % 4][(j // 4) * TOK : (j // 4 + 1) * TOK]

    p_high, p_low = split(p_scr[...])
    product = matmul(p_high, m_hl[...])
    update = product[:, :128] + (product[:, 128:] + matmul(p_low, m_hl[:, :128]))
    pair_tile = (pin + update).astype(BF16).astype(F32)
    normal = normalize(pair_tile)[0]
    n_high, n_low = split(normal)
    logits = matmul(n_high, score_high) + (matmul(n_high, score_low) + matmul(n_low, score_high))
    own = iota((TOK, 1, 128), 2) % TOK == iota((TOK, 1, 128), 0)
    logits = jnp.sum(jnp.where(own, logits.reshape(TOK, TOK, 128), 0.0), axis=0)
    lg_src[...] = jnp.where(valid > 0, logits, LOW)

    def send_plane(src, dst, phase):
        local(src, dst, phase)

        @pl.loop(1, N)
        def _(d):
            remote(src, dst, phase, (S + d) % N, T).start()

    send_plane(lg_src, lg_all.at[slot(S)], LOGITS)

    po_scr[...] = pair_tile
    for i in range(TOK):
        po_tile[i] = po_scr[pl.ds(i, TOK, stride=TOK), :].astype(BF16)

    @pl.when(y == col)
    def _():
        local(po_tile, po_mid, TURN)

    @pl.when(y != col)
    def _():
        remote(po_tile, po_mid, TURN, col * NC + xpos, row * NC + y).start()

    wait_recv(nv.at[half], NORM)
    remote(nv.at[half], nv.at[half], NORM_SIB, S, sibling).start()

    def values(start):
        @pl.loop(0, 4)
        def _(n):
            blocks = pl.ds(start + 2 * n, 2)
            rows = nv[blocks].reshape(2 * 8 * TOK, 256)
            vh[blocks] = matmul(rows, wc_blk[...]).astype(BF16).reshape(2, 8, TOK, 1024)

    values(core * (N // 2))

    wait_recv(po_mid, TURN)
    top, low = pl.ds(0, TOK // 2), pl.ds(TOK // 2, TOK // 2)
    across_x = pl.ds(xpos * TOK, TOK)
    own_a, own_b = po_all.at[y, top, across_x, :], po_all.at[y, low, across_x, :]
    local(po_mid.at[top], own_a, A1)
    local(po_mid.at[low], own_b, B1)
    for d in (1, 3, 2):
        remote(po_mid.at[top], own_a, A1, y * NC + (xpos + d) % NC, T).start()
        remote(po_mid.at[low], own_b, B1, (S + NC * d) % N, T).start()

    wait_recv(lg_all, LOGITS)
    lg = lg_all[...].reshape(2, 8, TOK, 128)
    parts = swap_blocks([lg[:, s].reshape(2 * TOK, 128) for s in range(8)], TOK)
    lg = jnp.stack([jnp.concatenate([a[:TOK], a[TOK:]], axis=1) for a in parts], axis=0)
    scaled = jnp.exp(lg - jnp.max(lg, axis=-1, keepdims=True))
    prob = scaled / jnp.sum(scaled, axis=-1, keepdims=True)
    prob_scr[...] = prob

    wait_recv(nv.at[other], NORM_SIB)
    values((1 - core) * (N // 2))

    def head(ref, h):
        return [ref[:, g, :, h * 128 : (h + 1) * 128].reshape(256, 128) for g in range(8)]

    gl = []
    for h in range(HEADS):
        gw = matmul_nt(
            jnp.concatenate([gbuf[g * TOK : (g + 1) * TOK, h * 128 : (h + 1) * 128] for g in range(8)], axis=1),
            jnp.concatenate(head(vh, h), axis=1),
        )
        prob = prob_scr[h]
        gl.append(prob * (gw - jnp.sum(prob * gw, axis=-1, keepdims=True)))
    parts = swap_blocks([jnp.concatenate([a[:, :128], a[:, 128:]], axis=0) for a in gl], TOK)
    for s in range(N):
        start = (s % 2) * TOK
        rsbuf[s] = parts[s // 2][start : start + TOK].astype(BF16)
    local(rsbuf.at[S], rsrx.at[S], GL_SUM)

    @pl.loop(1, N)
    def _(d):
        s = (S + d) % N
        remote(rsbuf.at[s], rsrx.at[S], GL_SUM, s, T).start()

    lines = po_all.at[y, top]
    wait_recv(lines, A1)
    for d in (1, 3, 2):
        remote(lines, lines, A2, (S + NC * d) % N, T).start()
    stripe = po_all.at[:, low, across_x, :]
    wait_recv(stripe, B1)
    for d in (1, 3, 2):
        remote(stripe, stripe, B2, y * NC + (xpos + d) % NC, T).start()

    weights = prob_scr[...].astype(BF16)
    columns = []
    for h in range(HEADS):
        avg = matmul(weights[h], jnp.concatenate(head(vh, h), axis=1))
        avg = jnp.concatenate([avg[:, g * 128 : (g + 1) * 128] for g in range(8)], axis=0)
        columns.append((avg * gate_scr[:, h * 128 : (h + 1) * 128]).astype(BF16))
    mixed = matmul_nt(jnp.concatenate(columns, axis=1), wf_blk[...])
    result = (by_group(x_ref[...].astype(F32)) + mixed).astype(BF16)
    for q in range(4):
        out_al[:, q] = result[:, q * FEAT : (q + 1) * FEAT].reshape(8, TOK, FEAT)

    wait_recv(rsrx, GL_SUM)
    gl_tile[...] = jnp.sum(rsrx[...].astype(F32), axis=0).astype(BF16)
    place = gl_all.at[col, xpos]
    owner = row * NC + y

    @pl.when(y == col)
    def _():
        local(gl_tile, place, GL)

    @pl.when(y != col)
    def _():
        remote(gl_tile, place, GL, S, owner).start()

    @pl.loop(1, N)
    def _(d):
        remote(gl_tile, place, GL, (S + d) % N, owner).start()

    wait_recv(po_all.at[pl.ds(0, 3), top], A2)
    wait_recv(po_all.at[pl.ds(0, 3), low], B2)
    po_copy = pltpu.make_async_copy(po_all, out_pair, local_sem.at[9])
    po_copy.start()
    wait_recv(gl_all, GL)
    out_gl[...] = gl_all[...]
    po_copy.wait()

    @pl.when(y == col)
    def _():
        wait_send(pair_hbm.at[pl.ds(0, 3 * TOK), pl.ds(0, TOK), :], PAIR_IN)
        wait_send(rsrx.at[pl.ds(0, 15)], GL)

    @pl.when(y != col)
    def _():
        wait_send(po_tile, TURN)
        wait_send(rsrx, GL)

    @pl.when(alone)
    def _():
        wait_send(r_all.at[pl.ds(0, 7)], RIGHT)

    @pl.when(jnp.logical_not(alone))
    def _():
        wait_send(r_all.at[pl.ds(0, 8)], RIGHT)

    wait_send(l_all.at[pl.ds(0, 15)], LEFT)
    wait_send(r_all.at[pl.ds(0, 8)], RIGHT_SIB)
    wait_send(nv.at[pl.ds(0, 7)], NORM)
    wait_send(nv.at[pl.ds(0, 8)], NORM_SIB)
    wait_send(lg_all.at[pl.ds(0, 15)], LOGITS)
    wait_send(po_all.at[0, pl.ds(0, 8), pl.ds(0, 48), :], A1)
    wait_send(po_all.at[0, pl.ds(0, 8), pl.ds(0, 48), :], B1)
    wait_send(po_all.at[pl.ds(0, 3), top], A2)
    wait_send(po_all.at[pl.ds(0, 3), low], B2)
    wait_send(rsrx.at[pl.ds(0, 15)], GL_SUM)


def finish_kernel(po_ref, gl_ref, score_ref, al_ref, out_al, out_pair, out_grad, gl_scr, c_hl):
    @pl.when(pl.program_id(0) == 0)
    def _():
        score = score_ref[...]
        repeat = jnp.where(iota((HEADS, 128), 1) // TOK == iota((HEADS, 128), 0), 1.0, 0.0).astype(BF16)
        high, low = split(score - jnp.mean(score, axis=1, keepdims=True))
        c_hl[:128] = matmul_tn(high, repeat).astype(BF16)
        c_hl[128:] = matmul_tn(low, repeat).astype(BF16)

    out_al[...] = al_ref[...]
    out_pair[...] = po_ref[...]
    for s in range(NC):
        gl_scr[:, s] = gl_ref[0, s].astype(F32).reshape(TOK, 1, 128)
    own = (iota((1, 1, TOK, 128), 3) % TOK) == iota((1, 1, TOK, 128), 2)
    part = TOK // 2
    for b in range(2):
        rows = pl.ds(b * part, part)
        normal, inverse = normalize(po_ref[rows].reshape(part * 64, 128).astype(F32))
        lhs = jnp.where(own, gl_scr[rows], 0.0).astype(BF16).reshape(part * 64, 128)
        grad = matmul_nt(lhs, c_hl[...])
        grad = grad[:, :128] + grad[:, 128:]
        along = jnp.mean(grad * normal, axis=-1, keepdims=True)
        out_grad[rows] = (inverse * (grad - normal * along)).astype(BF16).reshape(part, 64, 128)


def on_device(
    alignment_input,
    pair_input,
    token_valid_mask,
    first_factor_weights,
    second_factor_weights,
    content_weights_grid,
    sigmoid_weights_grid,
    outer_matrix,
    score_matrix,
    final_mixing_weights,
    adjoint_of_rowset,
):
    vmem = pl.BlockSpec(memory_space=pltpu.VMEM)
    smem = pl.BlockSpec(memory_space=pltpu.SMEM)
    hbm = pl.BlockSpec(memory_space=pltpu.HBM)
    V = pltpu.VMEM
    scratch = [
        V((8, 4, TOK, FEAT), BF16),
        V((8, 4, TOK, FEAT), BF16),
        V((32, FEAT), BF16),
        V((32, FEAT), BF16),
        V((FEAT, 256), BF16),
        V((FEAT, 256), BF16),
        V((FEAT, 256), BF16),
        V((HEADS, 128), F32),
        V((1024, 128), F32),
        V((SEQ * TOK, FEAT), F32),
        V((4, SEQ, 128), BF16),
        V((4, SEQ, 128), BF16),
        V((N, 4, SEQ, 128), BF16),
        V((N, 4, SEQ, 128), BF16),
        V((8, TOK, 256), BF16),
        V((N, 8, TOK, 256), BF16),
        V((N, 8, TOK, 1024), BF16),
        V((128, 1024), BF16),
        V((128, 1024), F32),
        V((256, 1024), BF16),
        V((256, 1024), BF16),
        V((1024, 256), BF16),
        V((TOK, TOK, 128), BF16),
        V((TOK * TOK, 128), F32),
        V((4, 512, 128), F32),
        V((256, 1024), F32),
        V((256, 128), F32),
        V((TOK, TOK, 128), BF16),
        V((TOK, TOK, 128), BF16),
        V((NC, TOK, 64, 128), BF16),
        V((TOK, 128), F32),
        V((N, TOK, 128), F32),
        V((HEADS, TOK, 256), F32),
        V((N, TOK, 128), BF16),
        V((N, TOK, 128), BF16),
        V((TOK, 128), BF16),
        V((NC, NC, TOK, 128), BF16),
        pltpu.SemaphoreType.DMA((PHASES,)),
        pltpu.SemaphoreType.DMA((PHASES,)),
        pltpu.SemaphoreType.DMA((10,)),
    ]
    grouped = (8, 4, TOK, FEAT)
    aligned, pair_block, grad_logits = pl.pallas_call(
        kernel,
        out_shape=[
            jax.ShapeDtypeStruct(grouped, BF16),
            jax.ShapeDtypeStruct((NC, TOK, 64, 128), BF16),
            jax.ShapeDtypeStruct((NC, NC, TOK, 128), BF16),
        ],
        in_specs=[smem] + [hbm] * 10,
        out_specs=[vmem, hbm, vmem],
        scratch_shapes=scratch,
        compiler_params=pltpu.CompilerParams(
            collective_id=0, has_side_effects=True, vmem_limit_bytes=60 * 1024 * 1024
        ),
        name="msa_block",
    )(
        token_valid_mask,
        alignment_input.reshape(grouped),
        adjoint_of_rowset.reshape(grouped),
        first_factor_weights.T,
        second_factor_weights.T,
        content_weights_grid,
        sigmoid_weights_grid,
        final_mixing_weights.T,
        score_matrix.T,
        outer_matrix,
        pair_input,
    )
    rows = pl.BlockSpec((TOK, 64, 128), lambda n: (n, 0, 0))
    groups = pl.BlockSpec((2, 4, TOK, FEAT), lambda n: (n, 0, 0, 0))
    aligned, pair_output, pair_gradient = pl.pallas_call(
        finish_kernel,
        grid=(NC,),
        out_shape=[
            jax.ShapeDtypeStruct(grouped, BF16),
            jax.ShapeDtypeStruct((64, 64, 128), BF16),
            jax.ShapeDtypeStruct((64, 64, 128), BF16),
        ],
        in_specs=[
            rows,
            pl.BlockSpec((1, NC, TOK, 128), lambda n: (n, 0, 0, 0)),
            pl.BlockSpec((HEADS, 128), lambda n: (0, 0)),
            groups,
        ],
        out_specs=[groups, rows, rows],
        scratch_shapes=[V((TOK, NC, 1, 128), F32), V((256, 128), BF16)],
        compiler_params=pltpu.CompilerParams(vmem_limit_bytes=60 * 1024 * 1024),
        name="pair_gradient",
    )(pair_block.reshape(64, 64, 128), grad_logits, score_matrix.T, aligned)
    return aligned.reshape(SEQ, TOK, FEAT), pair_output, pair_gradient


def solution(mesh):
    in_specs = (
        P("seq", ("row", "col"), None),
        P("row", "col", None),
        P(),
        P(),
        P(),
        P(),
        P(),
        P(),
        P(),
        P(),
        P("seq", ("row", "col"), None),
    )
    out_specs = (P("seq", ("row", "col"), None), P("row", "col", None), P("row", "col", None))
    return jax.shard_map(
        on_device, mesh=mesh, in_specs=in_specs, out_specs=out_specs, check_vma=False
    )
```

```python
import jax
import jax.numpy as jnp
from jax import lax
from jax.experimental import pallas as pl
from jax.experimental.pallas import tpu as pltpu
from jax.sharding import PartitionSpec as P

F32 = jnp.float32
BF16 = jnp.bfloat16
I32 = jnp.int32
EPS = 1e-05
LOW = -1e30
MESH = pl.DeviceIdType.MESH

N = 16
NC = 4
TOK = 16
SEQ = 32
HEADS = 8
FEAT = 64

PAIR_IN, LEFT, RIGHT, RIGHT_SIB, NORM, NORM_SIB, FAR, FAR_SIB, LOGITS, TURN, A1, B1, A2, B2, GL_SUM, GL = range(16)
PHASES = 16
FAR_FIRST = (10, 6, 14, 9, 11, 2, 8, 5, 7, 13, 15, 1, 3, 4, 12)


def iota(shape, dim):
    return lax.broadcasted_iota(I32, shape, dim)


def matmul(a, b):
    return jnp.dot(a, b, preferred_element_type=F32)


def matmul_nt(a, b):
    return lax.dot_general(a, b, (((1,), (1,)), ((), ())), preferred_element_type=F32)


def matmul_tn(a, b):
    return lax.dot_general(a, b, (((0,), (0,)), ((), ())), preferred_element_type=F32)


def split(a):
    high = a.astype(BF16)
    return high, (a - high.astype(F32)).astype(BF16)


def normalize(a):
    center = a - jnp.mean(a, axis=-1, keepdims=True)
    inverse = lax.rsqrt(jnp.mean(center * center, axis=-1, keepdims=True) + EPS)
    return center * inverse, inverse


def swap_blocks(arrays, width):
    arrays = list(arrays)
    lanes = arrays[0].shape[1]
    block = iota(arrays[0].shape, 1) // width
    bit = len(arrays) // 2
    while bit:
        upper = (block & bit) != 0
        for low in range(len(arrays)):
            if low & bit:
                continue
            a, b = arrays[low], arrays[low | bit]
            arrays[low] = jnp.where(upper, pltpu.roll(b, bit * width, 1), a)
            arrays[low | bit] = jnp.where(upper, b, pltpu.roll(a, lanes - bit * width, 1))
        bit //= 2
    return arrays


def kernel(
    mask_s, x_hbm, adj_hbm, w1_hbm, w2_hbm, wc_hbm, ws_hbm, wf_hbm, score_hbm, m_hbm, pair_hbm,
    out_al, out_pair, out_gl,
    x_ref, adj_ref, w1_ref, w2_ref, wc_ref, ws_ref, wf_ref, score_ref, m_scr,
    xn_scr, lbuf, rbuf, l_all, r_all, nbuf, nv, vh, gbuf, gate_scr, wc_blk, wf_blk, m_hl,
    pin_tile, pin_scr, o_scr, p_scr, po_scr, po_tile, po_mid, po_all, lg_src, lg_all, prob_scr,
    rsbuf, rsrx, gl_tile, gl_all,
    send_sem, recv_sem, local_sem,
):
    S = lax.axis_index("seq")
    row = lax.axis_index("row")
    col = lax.axis_index("col")
    T = row * NC + col
    y = S // NC
    xpos = S % NC
    core = T % 2
    sibling = T + 1 - 2 * core

    def slot(n):
        return (n % 2) * (N // 2) + n // 2

    def device(s, t):
        return (s, t // NC, t % NC)

    def remote(src, dst, phase, s, t):
        return pltpu.make_async_remote_copy(
            src_ref=src, dst_ref=dst, send_sem=send_sem.at[phase], recv_sem=recv_sem.at[phase],
            device_id=device(s, t), device_id_type=MESH,
        )

    def local(src, dst, phase):
        pltpu.make_async_copy(src, dst, recv_sem.at[phase]).start()

    def wait_recv(buf, phase):
        pltpu.make_async_copy(buf, buf, recv_sem.at[phase]).wait()

    def wait_send(buf, phase):
        pltpu.make_async_copy(buf, buf, send_sem.at[phase]).wait()

    loads = []

    def load(*pairs):
        for src, dst in pairs:
            copy = pltpu.make_async_copy(src, dst, local_sem.at[len(loads)])
            copy.start()
            loads.append(copy)

    load((x_hbm, x_ref), (w1_hbm, w1_ref), (w2_hbm, w2_ref))
    load(
        (wc_hbm, wc_ref), (ws_hbm, ws_ref), (wf_hbm, wf_ref), (adj_hbm, adj_ref), (score_hbm, score_ref), (m_hbm, m_scr)
    )


    plane_x = [(xpos + d) % NC for d in range(NC)]
    plane_y = [(y + d) % NC * NC for d in range(NC)]

    def plane(d):
        return plane_y[d // NC] + plane_x[d % NC]

    barrier = pltpu.get_barrier_semaphore()

    def greet(s, t):
        pl.semaphore_signal(barrier, inc=1, device_id=device(s, t), device_id_type=MESH)

    for d in range(1, N):
        greet((S + d) % N, T)
    for d in range(1, N // 2):
        greet(S, (T + 2 * d) % N)
    greet(S, sibling)
    across = (sibling + 2) % 4
    greet(S, row * NC + across)

    def right_source(d):
        return (core + 2 * d + 2 * (S // 2)) % N

    for d in range(1, N // 2):
        greet(right_source(d), S)

    @pl.when(jnp.logical_or(right_source(0) != S, S != T))
    def _():
        greet(right_source(0), S)

    alone = jnp.logical_and(S == T, S % 2 == core)
    greeted = N - 1 + N // 2 - 1 + 2 + N // 2 - jnp.where(alone, 1, 0).astype(I32)

    loads[0].wait()
    xn = normalize(x_ref[...].reshape(SEQ * TOK, FEAT).astype(F32))[0].astype(BF16).astype(F32)
    xn_scr[...] = xn

    def by_group(a):
        a = a.reshape(8, 4, TOK, FEAT)
        return jnp.concatenate([a[:, q].reshape(8 * TOK, FEAT) for q in range(4)], axis=1)

    loads[1].wait()
    loads[2].wait()
    lane = iota((32, 256), 1)
    chan = iota((32, 256), 0)
    same = lane % 32 == chan
    pick_left = jnp.where(jnp.logical_and(same, lane < 128), 1.0, 0.0).astype(BF16)
    pick_right = jnp.where(jnp.logical_and(same, lane >= 128), 1.0, 0.0).astype(BF16)
    both = matmul_tn(w1_ref[...], pick_left) + matmul_tn(w2_ref[...], pick_right)
    quarter = (iota((FEAT, 256), 1) // 32) % 4
    w_lr = jnp.concatenate([jnp.where(quarter == q, both, 0.0) for q in range(4)], axis=0).astype(BF16)
    x_lr = []
    for q in range(4):
        parts = []
        for group in range(4):
            token = 4 * group + q
            parts.append(
                xn_scr[pl.ds(token, SEQ, stride=TOK), :] * mask_s[T * TOK + token].astype(F32)
            )
        x_lr.append(jnp.concatenate(parts, axis=0))
    factors = matmul(jnp.concatenate(x_lr, axis=1).astype(BF16), w_lr).astype(BF16)
    lbuf[...] = factors[:, :128].reshape(4, SEQ, 128)
    rbuf[...] = factors[:, 128:].reshape(4, SEQ, 128)

    pl.semaphore_wait(barrier, greeted)

    parity = S % 2

    def send_right(d):
        remote(rbuf, r_all.at[slot(S)], RIGHT, T, (T - core + parity + 2 * d) % N).start()

    for d in (4, 3, 5, 2, 6, 1, 7):
        send_right(d)

    @pl.when(alone)
    def _():
        local(rbuf, r_all.at[slot(S)], RIGHT)

    @pl.when(jnp.logical_not(alone))
    def _():
        send_right(0)

    local(lbuf, l_all.at[slot(S)], LEFT)

    for d in FAR_FIRST:
        remote(lbuf, l_all.at[slot(S)], LEFT, plane(d), T).start()

    my_tile = pair_hbm.at[pl.ds(col * TOK, TOK), pl.ds(xpos * TOK, TOK), :]

    @pl.when(y == col)
    def _():
        local(my_tile, pin_tile, PAIR_IN)

        @pl.loop(1, NC)
        def _(d):
            c = (col + d) % NC
            remote(
                pair_hbm.at[pl.ds(c * TOK, TOK), pl.ds(xpos * TOK, TOK), :], pin_tile, PAIR_IN, S, row * NC + c
            ).start()

    x_v = by_group(xn).astype(BF16)
    nbuf[...] = x_v.reshape(8, TOK, 256)
    local(nbuf, nv.at[slot(T)], NORM)
    for d in (2, 6, 1, 7):
        remote(nbuf, nv.at[slot(T)], NORM, S, (T + 2 * d) % N).start()

    lane = iota((256, 1024), 1)
    chan = iota((256, 1024), 0)
    pick = jnp.where(
        jnp.logical_and(lane // 128 == chan // 32, lane % 32 == chan % 32), 1.0, 0.0
    ).astype(BF16)
    quarter = (iota((FEAT, 1024), 1) // 32) % 4

    def spread(w):
        return jnp.concatenate([jnp.where(quarter == q, w, 0.0) for q in range(4)], axis=0).astype(BF16)

    loads[3].wait()
    wc_blk[...] = spread(matmul(wc_ref[...], pick))

    loads[4].wait()
    gate = jax.nn.sigmoid(matmul(x_v, spread(matmul(ws_ref[...], pick))))
    gate_scr[...] = gate
    loads[5].wait()
    wf_blk[...] = spread(matmul(wf_ref[...], pick))
    loads[6].wait()
    x_g = by_group(adj_ref[...].astype(F32)).astype(BF16)
    gbuf[...] = (matmul(x_g, wf_blk[...]) * gate).astype(BF16)

    loads[7].wait()
    loads[8].wait()
    m_high, m_low = split(m_scr[...])
    m_hl[:, :128] = m_high
    m_hl[:, 128:] = m_low
    score = score_ref[...]
    repeat = jnp.where(iota((HEADS, 128), 1) // TOK == iota((HEADS, 128), 0), 1.0, 0.0).astype(BF16)

    def repeated(a):
        high, low = split(a)
        return matmul_tn(high, repeat).astype(BF16), matmul_tn(low, repeat).astype(BF16)

    score_high, score_low = repeated(score)
    lane = iota((1, 128), 1) % TOK
    valid = jnp.zeros((1, 128), F32)
    for j in range(TOK):
        valid = jnp.where(lane == j, mask_s[S * TOK + j].astype(F32), valid)
    wait_recv(pin_tile, PAIR_IN)
    pin_scr[...] = pin_tile[...].reshape(TOK * TOK, 128).astype(F32)
    pin = jnp.concatenate([pin_scr[pl.ds(j, TOK, stride=TOK), :] for j in range(TOK)], axis=0)

    half = pl.ds(core * (N // 2), N // 2)
    other = pl.ds((1 - core) * (N // 2), N // 2)
    wait_recv(r_all.at[half], RIGHT)
    remote(r_all.at[half], r_all.at[half], RIGHT_SIB, S, sibling).start()

    def factors_of(ref, part):
        return jnp.concatenate([ref[part, g].reshape(N // 2 * SEQ, 128) for g in range(4)], axis=1)

    wait_recv(l_all, LEFT)
    outer = matmul_tn(factors_of(l_all, half), factors_of(r_all, half))
    wait_recv(r_all.at[other], RIGHT_SIB)
    outer += matmul_tn(factors_of(l_all, other), factors_of(r_all, other))
    for g in range(4):
        o_scr[g] = outer[:, g * 128 : (g + 1) * 128]

    @pl.loop(0, 8, unroll=True)
    def _(cg):
        parts = [
            jnp.concatenate([o_scr[g, pl.ds(4 * cg + q, TOK, stride=32), :] for g in range(4)], axis=0)
            for q in range(4)
        ]
        parts = swap_blocks(parts, 32)
        lanes = pl.ds(pl.multiple_of(cg * 128, 128), 128)
        for j in range(TOK):
            p_scr[pl.ds(j * TOK, TOK), lanes] = parts[j % 4][(j // 4) * TOK : (j // 4 + 1) * TOK]

    p_high, p_low = split(p_scr[...])
    product = matmul(p_high, m_hl[...])
    update = product[:, :128] + (product[:, 128:] + matmul(p_low, m_hl[:, :128]))
    pair_tile = (pin + update).astype(BF16).astype(F32)
    normal = normalize(pair_tile)[0]
    n_high, n_low = split(normal)
    logits = matmul(n_high, score_high) + (matmul(n_high, score_low) + matmul(n_low, score_high))
    own = iota((TOK, 1, 128), 2) % TOK == iota((TOK, 1, 128), 0)
    logits = jnp.sum(jnp.where(own, logits.reshape(TOK, TOK, 128), 0.0), axis=0)
    lg_src[...] = jnp.where(valid > 0, logits, LOW)

    def send_plane(src, dst, phase):
        for d in FAR_FIRST:
            remote(src, dst, phase, plane(d), T).start()
        local(src, dst, phase)

    send_plane(lg_src, lg_all.at[slot(S)], LOGITS)

    po_scr[...] = pair_tile
    for i in range(TOK):
        po_tile[i] = po_scr[pl.ds(i, TOK, stride=TOK), :].astype(BF16)

    @pl.when(y == col)
    def _():
        local(po_tile, po_mid, TURN)

    @pl.when(y != col)
    def _():
        remote(po_tile, po_mid, TURN, col * NC + xpos, row * NC + y).start()

    chip = T // 2

    def place(d, swap=0):
        c = core + swap - 2 * swap * core
        return c * (N // 2) + (chip + d) % (N // 2)

    wait_recv(nv.at[pl.ds(0, 5)], NORM)
    for d, far in ((6, 2), (6, 1), (2, 7)):
        block = nv.at[place(d)]
        remote(block, block, FAR, S, (T + 2 * far) % N).start()
    near = (0, 1, 2, 6, 7)
    for d in near:
        block = nv.at[place(d)]
        remote(block, block, NORM_SIB, S, sibling).start()

    wait_recv(po_mid, TURN)
    top, low = pl.ds(0, TOK // 2), pl.ds(TOK // 2, TOK // 2)
    across_x = pl.ds(xpos * TOK, TOK)
    own_a, own_b = po_all.at[y, top, across_x, :], po_all.at[y, low, across_x, :]
    local(po_mid.at[top], own_a, A1)
    local(po_mid.at[low], own_b, B1)
    for d in (1, 3, 2):
        remote(po_mid.at[top], own_a, A1, y * NC + (xpos + d) % NC, T).start()
        remote(po_mid.at[low], own_b, B1, (S + NC * d) % N, T).start()

    def values(blocks):
        for n in blocks:
            vh[n] = matmul(nv[n].reshape(8 * TOK, 256), wc_blk[...]).astype(BF16).reshape(8, TOK, 1024)

    values([place(d) for d in near])
    wait_recv(nv.at[pl.ds(0, 5)], NORM_SIB)
    values([place(d, 1) for d in near])

    wait_recv(lg_all, LOGITS)
    lg = lg_all[...].reshape(2, 8, TOK, 128)
    parts = swap_blocks([lg[:, s].reshape(2 * TOK, 128) for s in range(8)], TOK)
    lg = jnp.stack([jnp.concatenate([a[:TOK], a[TOK:]], axis=1) for a in parts], axis=0)
    scaled = jnp.exp(lg - jnp.max(lg, axis=-1, keepdims=True))
    prob = scaled / jnp.sum(scaled, axis=-1, keepdims=True)
    prob_scr[...] = prob

    away = (3, 4, 5)
    wait_recv(nv.at[pl.ds(0, 3)], FAR)
    for d in away:
        block = nv.at[place(d)]
        remote(block, block, FAR_SIB, S, sibling).start()
    values([place(d) for d in away])
    wait_recv(nv.at[pl.ds(0, 3)], FAR_SIB)
    values([place(d, 1) for d in away])

    def head(ref, h):
        return [ref[:, g, :, h * 128 : (h + 1) * 128].reshape(256, 128) for g in range(8)]

    gl = []
    for h in range(HEADS):
        gw = matmul_nt(
            jnp.concatenate([gbuf[g * TOK : (g + 1) * TOK, h * 128 : (h + 1) * 128] for g in range(8)], axis=1),
            jnp.concatenate(head(vh, h), axis=1),
        )
        prob = prob_scr[h]
        gl.append(prob * (gw - jnp.sum(prob * gw, axis=-1, keepdims=True)))
    parts = swap_blocks([jnp.concatenate([a[:, :128], a[:, 128:]], axis=0) for a in gl], TOK)
    for s in range(N):
        start = (s % 2) * TOK
        rsbuf[s] = parts[s // 2][start : start + TOK].astype(BF16)
    local(rsbuf.at[S], rsrx.at[S], GL_SUM)

    for d in FAR_FIRST:
        s = plane(d)
        remote(rsbuf.at[s], rsrx.at[S], GL_SUM, s, T).start()

    lines = po_all.at[y, top]
    wait_recv(lines, A1)
    for d in (1, 3, 2):
        remote(lines, lines, A2, (S + NC * d) % N, T).start()
    stripe = po_all.at[:, low, across_x, :]
    wait_recv(stripe, B1)
    for d in (1, 3, 2):
        remote(stripe, stripe, B2, y * NC + (xpos + d) % NC, T).start()

    weights = prob_scr[...].astype(BF16)
    columns = []
    for h in range(HEADS):
        avg = matmul(weights[h], jnp.concatenate(head(vh, h), axis=1))
        avg = jnp.concatenate([avg[:, g * 128 : (g + 1) * 128] for g in range(8)], axis=0)
        columns.append((avg * gate_scr[:, h * 128 : (h + 1) * 128]).astype(BF16))
    mixed = matmul_nt(jnp.concatenate(columns, axis=1), wf_blk[...])
    result = (by_group(x_ref[...].astype(F32)) + mixed).astype(BF16)
    for q in range(4):
        out_al[:, q] = result[:, q * FEAT : (q + 1) * FEAT].reshape(8, TOK, FEAT)

    wait_recv(rsrx, GL_SUM)
    gl_tile[...] = jnp.sum(rsrx[...].astype(F32), axis=0).astype(BF16)
    target = gl_all.at[col, xpos]
    owner = row * NC + y

    @pl.when(y == col)
    def _():
        local(gl_tile, target, GL)

    @pl.when(y != col)
    def _():
        remote(gl_tile, target, GL, S, owner).start()

    for d in FAR_FIRST:
        remote(gl_tile, target, GL, plane(d), owner).start()

    wait_recv(po_all.at[pl.ds(0, 3), top], A2)
    wait_recv(po_all.at[pl.ds(0, 3), low], B2)
    po_copy = pltpu.make_async_copy(po_all, out_pair, local_sem.at[9])
    po_copy.start()
    wait_recv(gl_all, GL)
    out_gl[...] = gl_all[...]
    po_copy.wait()

    @pl.when(y == col)
    def _():
        wait_send(pair_hbm.at[pl.ds(0, 3 * TOK), pl.ds(0, TOK), :], PAIR_IN)
        wait_send(rsrx.at[pl.ds(0, 15)], GL)

    @pl.when(y != col)
    def _():
        wait_send(po_tile, TURN)
        wait_send(rsrx, GL)

    @pl.when(alone)
    def _():
        wait_send(r_all.at[pl.ds(0, 7)], RIGHT)

    @pl.when(jnp.logical_not(alone))
    def _():
        wait_send(r_all.at[pl.ds(0, 8)], RIGHT)

    wait_send(l_all.at[pl.ds(0, 15)], LEFT)
    wait_send(r_all.at[pl.ds(0, 8)], RIGHT_SIB)
    wait_send(nv.at[pl.ds(0, 4)], NORM)
    wait_send(nv.at[pl.ds(0, 5)], NORM_SIB)
    wait_send(nv.at[pl.ds(0, 3)], FAR)
    wait_send(nv.at[pl.ds(0, 3)], FAR_SIB)
    wait_send(lg_all.at[pl.ds(0, 15)], LOGITS)
    wait_send(po_all.at[0, pl.ds(0, 8), pl.ds(0, 48), :], A1)
    wait_send(po_all.at[0, pl.ds(0, 8), pl.ds(0, 48), :], B1)
    wait_send(po_all.at[pl.ds(0, 3), top], A2)
    wait_send(po_all.at[pl.ds(0, 3), low], B2)
    wait_send(rsrx.at[pl.ds(0, 15)], GL_SUM)


def finish_kernel(po_ref, gl_ref, score_ref, al_ref, out_al, out_pair, out_grad, gl_scr, c_hl):
    @pl.when(pl.program_id(0) == 0)
    def _():
        score = score_ref[...]
        repeat = jnp.where(iota((HEADS, 128), 1) // TOK == iota((HEADS, 128), 0), 1.0, 0.0).astype(BF16)
        high, low = split(score - jnp.mean(score, axis=1, keepdims=True))
        c_hl[:128] = matmul_tn(high, repeat).astype(BF16)
        c_hl[128:] = matmul_tn(low, repeat).astype(BF16)

    out_al[...] = al_ref[...]
    out_pair[...] = po_ref[...]
    for s in range(NC):
        gl_scr[:, s] = gl_ref[0, s].astype(F32).reshape(TOK, 1, 128)
    own = (iota((1, 1, TOK, 128), 3) % TOK) == iota((1, 1, TOK, 128), 2)
    part = TOK // 2
    for b in range(2):
        rows = pl.ds(b * part, part)
        normal, inverse = normalize(po_ref[rows].reshape(part * 64, 128).astype(F32))
        lhs = jnp.where(own, gl_scr[rows], 0.0).astype(BF16).reshape(part * 64, 128)
        grad = matmul_nt(lhs, c_hl[...])
        grad = grad[:, :128] + grad[:, 128:]
        along = jnp.mean(grad * normal, axis=-1, keepdims=True)
        out_grad[rows] = (inverse * (grad - normal * along)).astype(BF16).reshape(part, 64, 128)


def on_device(
    alignment_input,
    pair_input,
    token_valid_mask,
    first_factor_weights,
    second_factor_weights,
    content_weights_grid,
    sigmoid_weights_grid,
    outer_matrix,
    score_matrix,
    final_mixing_weights,
    adjoint_of_rowset,
):
    vmem = pl.BlockSpec(memory_space=pltpu.VMEM)
    smem = pl.BlockSpec(memory_space=pltpu.SMEM)
    hbm = pl.BlockSpec(memory_space=pltpu.HBM)
    V = pltpu.VMEM
    scratch = [
        V((8, 4, TOK, FEAT), BF16),
        V((8, 4, TOK, FEAT), BF16),
        V((32, FEAT), BF16),
        V((32, FEAT), BF16),
        V((FEAT, 256), BF16),
        V((FEAT, 256), BF16),
        V((FEAT, 256), BF16),
        V((HEADS, 128), F32),
        V((1024, 128), F32),
        V((SEQ * TOK, FEAT), F32),
        V((4, SEQ, 128), BF16),
        V((4, SEQ, 128), BF16),
        V((N, 4, SEQ, 128), BF16),
        V((N, 4, SEQ, 128), BF16),
        V((8, TOK, 256), BF16),
        V((N, 8, TOK, 256), BF16),
        V((N, 8, TOK, 1024), BF16),
        V((128, 1024), BF16),
        V((128, 1024), F32),
        V((256, 1024), BF16),
        V((256, 1024), BF16),
        V((1024, 256), BF16),
        V((TOK, TOK, 128), BF16),
        V((TOK * TOK, 128), F32),
        V((4, 512, 128), F32),
        V((256, 1024), F32),
        V((256, 128), F32),
        V((TOK, TOK, 128), BF16),
        V((TOK, TOK, 128), BF16),
        V((NC, TOK, 64, 128), BF16),
        V((TOK, 128), F32),
        V((N, TOK, 128), F32),
        V((HEADS, TOK, 256), F32),
        V((N, TOK, 128), BF16),
        V((N, TOK, 128), BF16),
        V((TOK, 128), BF16),
        V((NC, NC, TOK, 128), BF16),
        pltpu.SemaphoreType.DMA((PHASES,)),
        pltpu.SemaphoreType.DMA((PHASES,)),
        pltpu.SemaphoreType.DMA((10,)),
    ]
    grouped = (8, 4, TOK, FEAT)
    aligned, pair_block, grad_logits = pl.pallas_call(
        kernel,
        out_shape=[
            jax.ShapeDtypeStruct(grouped, BF16),
            jax.ShapeDtypeStruct((NC, TOK, 64, 128), BF16),
            jax.ShapeDtypeStruct((NC, NC, TOK, 128), BF16),
        ],
        in_specs=[smem] + [hbm] * 10,
        out_specs=[vmem, hbm, vmem],
        scratch_shapes=scratch,
        compiler_params=pltpu.CompilerParams(
            collective_id=0, has_side_effects=True, vmem_limit_bytes=60 * 1024 * 1024
        ),
        name="msa_block",
    )(
        token_valid_mask,
        alignment_input.reshape(grouped),
        adjoint_of_rowset.reshape(grouped),
        first_factor_weights.T,
        second_factor_weights.T,
        content_weights_grid,
        sigmoid_weights_grid,
        final_mixing_weights.T,
        score_matrix.T,
        outer_matrix,
        pair_input,
    )
    rows = pl.BlockSpec((TOK, 64, 128), lambda n: (n, 0, 0))
    groups = pl.BlockSpec((2, 4, TOK, FEAT), lambda n: (n, 0, 0, 0))
    aligned, pair_output, pair_gradient = pl.pallas_call(
        finish_kernel,
        grid=(NC,),
        out_shape=[
            jax.ShapeDtypeStruct(grouped, BF16),
            jax.ShapeDtypeStruct((64, 64, 128), BF16),
            jax.ShapeDtypeStruct((64, 64, 128), BF16),
        ],
        in_specs=[
            rows,
            pl.BlockSpec((1, NC, TOK, 128), lambda n: (n, 0, 0, 0)),
            pl.BlockSpec((HEADS, 128), lambda n: (0, 0)),
            groups,
        ],
        out_specs=[groups, rows, rows],
        scratch_shapes=[V((TOK, NC, 1, 128), F32), V((256, 128), BF16)],
        compiler_params=pltpu.CompilerParams(vmem_limit_bytes=60 * 1024 * 1024),
        name="pair_gradient",
    )(pair_block.reshape(64, 64, 128), grad_logits, score_matrix.T, aligned)
    return aligned.reshape(SEQ, TOK, FEAT), pair_output, pair_gradient


def solution(mesh):
    in_specs = (
        P("seq", ("row", "col"), None),
        P("row", "col", None),
        P(),
        P(),
        P(),
        P(),
        P(),
        P(),
        P(),
        P(),
        P("seq", ("row", "col"), None),
    )
    out_specs = (P("seq", ("row", "col"), None), P("row", "col", None), P("row", "col", None))
    return jax.shard_map(
        on_device, mesh=mesh, in_specs=in_specs, out_specs=out_specs, check_vma=False
    )
```

```python
import jax
import jax.numpy as jnp
from jax import lax
from jax.experimental import pallas as pl
from jax.experimental.pallas import tpu as pltpu
from jax.sharding import PartitionSpec as P

F32 = jnp.float32
BF16 = jnp.bfloat16
I32 = jnp.int32
EPS = 1e-05
LOW = -1e30
MESH = pl.DeviceIdType.MESH

N = 16
NC = 4
TOK = 16
SEQ = 32
HEADS = 8
FEAT = 64

PAIR_IN, LEFT, RIGHT, RIGHT_SIB, NORM, NORM_SIB, FAR, FAR_SIB, LOGITS, TURN, A1, B1, A2, B2, GL_SUM, GL = range(16)
PHASES = 16
FAR_FIRST = (10, 6, 14, 9, 11, 2, 8, 5, 7, 13, 15, 1, 3, 4, 12)


def iota(shape, dim):
    return lax.broadcasted_iota(I32, shape, dim)


def matmul(a, b):
    return jnp.dot(a, b, preferred_element_type=F32)


def matmul_nt(a, b):
    return lax.dot_general(a, b, (((1,), (1,)), ((), ())), preferred_element_type=F32)


def matmul_tn(a, b):
    return lax.dot_general(a, b, (((0,), (0,)), ((), ())), preferred_element_type=F32)


def split(a):
    high = a.astype(BF16)
    return high, (a - high.astype(F32)).astype(BF16)


def normalize(a):
    center = a - jnp.mean(a, axis=-1, keepdims=True)
    inverse = lax.rsqrt(jnp.mean(center * center, axis=-1, keepdims=True) + EPS)
    return center * inverse, inverse


def swap_blocks(arrays, width):
    arrays = list(arrays)
    lanes = arrays[0].shape[1]
    block = iota(arrays[0].shape, 1) // width
    bit = len(arrays) // 2
    while bit:
        upper = (block & bit) != 0
        for low in range(len(arrays)):
            if low & bit:
                continue
            a, b = arrays[low], arrays[low | bit]
            arrays[low] = jnp.where(upper, pltpu.roll(b, bit * width, 1), a)
            arrays[low | bit] = jnp.where(upper, b, pltpu.roll(a, lanes - bit * width, 1))
        bit //= 2
    return arrays


def kernel(
    mask_s, x_hbm, adj_hbm, w1_hbm, w2_hbm, wc_hbm, ws_hbm, wf_hbm, score_hbm, m_hbm, pair_hbm,
    out_al, out_pair, out_gl,
    x_ref, adj_ref, w1_ref, w2_ref, wc_ref, ws_ref, wf_ref, score_ref, m_scr,
    xn_scr, lbuf, rbuf, l_all, r_all, nbuf, nv, vh, gbuf, gate_scr, wc_blk, wf_blk, m_hl,
    pin_tile, pin_scr, o_scr, p_scr, po_scr, po_tile, po_mid, po_all, lg_src, lg_all, prob_scr,
    al_scr, rsbuf, rsrx, gl_tile, gl_all,
    send_sem, recv_sem, local_sem,
):
    S = lax.axis_index("seq")
    row = lax.axis_index("row")
    col = lax.axis_index("col")
    T = row * NC + col
    y = S // NC
    xpos = S % NC
    core = T % 2
    sibling = T + 1 - 2 * core

    def slot(n):
        return (n % 2) * (N // 2) + n // 2

    def device(s, t):
        return (s, t // NC, t % NC)

    def remote(src, dst, phase, s, t):
        return pltpu.make_async_remote_copy(
            src_ref=src, dst_ref=dst, send_sem=send_sem.at[phase], recv_sem=recv_sem.at[phase],
            device_id=device(s, t), device_id_type=MESH,
        )

    def local(src, dst, phase):
        pltpu.make_async_copy(src, dst, recv_sem.at[phase]).start()

    def wait_recv(buf, phase):
        pltpu.make_async_copy(buf, buf, recv_sem.at[phase]).wait()

    def wait_send(buf, phase):
        pltpu.make_async_copy(buf, buf, send_sem.at[phase]).wait()

    loads = []

    def load(*pairs):
        for src, dst in pairs:
            copy = pltpu.make_async_copy(src, dst, local_sem.at[len(loads)])
            copy.start()
            loads.append(copy)

    load((x_hbm, x_ref), (w1_hbm, w1_ref), (w2_hbm, w2_ref))
    load(
        (wc_hbm, wc_ref), (ws_hbm, ws_ref), (wf_hbm, wf_ref), (adj_hbm, adj_ref), (score_hbm, score_ref), (m_hbm, m_scr)
    )


    plane_x = [(xpos + d) % NC for d in range(NC)]
    plane_y = [(y + d) % NC * NC for d in range(NC)]

    def plane(d):
        return plane_y[d // NC] + plane_x[d % NC]

    barrier = pltpu.get_barrier_semaphore()

    def greet(s, t):
        pl.semaphore_signal(barrier, inc=1, device_id=device(s, t), device_id_type=MESH)

    for d in range(1, N):
        greet((S + d) % N, T)
    for d in range(1, N // 2):
        greet(S, (T + 2 * d) % N)
    greet(S, sibling)
    across = (sibling + 2) % 4
    greet(S, row * NC + across)

    def right_source(d):
        return (core + 2 * d + 2 * (S // 2)) % N

    for d in range(1, N // 2):
        greet(right_source(d), S)

    @pl.when(jnp.logical_or(right_source(0) != S, S != T))
    def _():
        greet(right_source(0), S)

    alone = jnp.logical_and(S == T, S % 2 == core)
    greeted = N - 1 + N // 2 - 1 + 2 + N // 2 - jnp.where(alone, 1, 0).astype(I32)

    loads[0].wait()
    xn = normalize(x_ref[...].reshape(SEQ * TOK, FEAT).astype(F32))[0].astype(BF16).astype(F32)
    xn_scr[...] = xn

    def by_group(a):
        a = a.reshape(8, 4, TOK, FEAT)
        return jnp.concatenate([a[:, q].reshape(8 * TOK, FEAT) for q in range(4)], axis=1)

    loads[1].wait()
    loads[2].wait()
    lane = iota((32, 256), 1)
    chan = iota((32, 256), 0)
    same = lane % 32 == chan
    pick_left = jnp.where(jnp.logical_and(same, lane < 128), 1.0, 0.0).astype(BF16)
    pick_right = jnp.where(jnp.logical_and(same, lane >= 128), 1.0, 0.0).astype(BF16)
    both = matmul_tn(w1_ref[...], pick_left) + matmul_tn(w2_ref[...], pick_right)
    quarter = (iota((FEAT, 256), 1) // 32) % 4
    w_lr = jnp.concatenate([jnp.where(quarter == q, both, 0.0) for q in range(4)], axis=0).astype(BF16)
    x_lr = []
    for q in range(4):
        parts = []
        for group in range(4):
            token = 4 * group + q
            parts.append(
                xn_scr[pl.ds(token, SEQ, stride=TOK), :] * mask_s[T * TOK + token].astype(F32)
            )
        x_lr.append(jnp.concatenate(parts, axis=0))
    factors = matmul(jnp.concatenate(x_lr, axis=1).astype(BF16), w_lr).astype(BF16)
    lbuf[...] = factors[:, :128].reshape(4, SEQ, 128)
    rbuf[...] = factors[:, 128:].reshape(4, SEQ, 128)

    pl.semaphore_wait(barrier, greeted)

    parity = S % 2

    def send_right(d):
        remote(rbuf, r_all.at[slot(S)], RIGHT, T, (T - core + parity + 2 * d) % N).start()

    for d in (4, 3, 5, 2, 6, 1, 7):
        send_right(d)

    @pl.when(alone)
    def _():
        local(rbuf, r_all.at[slot(S)], RIGHT)

    @pl.when(jnp.logical_not(alone))
    def _():
        send_right(0)

    local(lbuf, l_all.at[slot(S)], LEFT)

    for d in FAR_FIRST:
        remote(lbuf, l_all.at[slot(S)], LEFT, plane(d), T).start()

    my_tile = pair_hbm.at[pl.ds(col * TOK, TOK), pl.ds(xpos * TOK, TOK), :]

    @pl.when(y == col)
    def _():
        local(my_tile, pin_tile, PAIR_IN)

        @pl.loop(1, NC)
        def _(d):
            c = (col + d) % NC
            remote(
                pair_hbm.at[pl.ds(c * TOK, TOK), pl.ds(xpos * TOK, TOK), :], pin_tile, PAIR_IN, S, row * NC + c
            ).start()

    x_v = by_group(xn).astype(BF16)
    nbuf[...] = x_v.reshape(8, TOK, 256)
    local(nbuf, nv.at[slot(T)], NORM)
    for d in (2, 6, 1, 7):
        remote(nbuf, nv.at[slot(T)], NORM, S, (T + 2 * d) % N).start()

    lane = iota((256, 1024), 1)
    chan = iota((256, 1024), 0)
    pick = jnp.where(
        jnp.logical_and(lane // 128 == chan // 32, lane % 32 == chan % 32), 1.0, 0.0
    ).astype(BF16)
    quarter = (iota((FEAT, 1024), 1) // 32) % 4

    def spread(w):
        return jnp.concatenate([jnp.where(quarter == q, w, 0.0) for q in range(4)], axis=0).astype(BF16)

    loads[3].wait()
    wc_blk[...] = spread(matmul(wc_ref[...], pick))

    loads[4].wait()
    gate = jax.nn.sigmoid(matmul(x_v, spread(matmul(ws_ref[...], pick))))
    gate_scr[...] = gate
    loads[5].wait()
    wf_blk[...] = spread(matmul(wf_ref[...], pick))
    loads[6].wait()
    x_g = by_group(adj_ref[...].astype(F32)).astype(BF16)
    gbuf[...] = (matmul(x_g, wf_blk[...]) * gate).astype(BF16)

    loads[7].wait()
    loads[8].wait()
    m_high, m_low = split(m_scr[...])
    m_hl[:, :128] = m_high
    m_hl[:, 128:] = m_low
    score = score_ref[...]
    repeat = jnp.where(iota((HEADS, 128), 1) // TOK == iota((HEADS, 128), 0), 1.0, 0.0).astype(BF16)

    def repeated(a):
        high, low = split(a)
        return matmul_tn(high, repeat).astype(BF16), matmul_tn(low, repeat).astype(BF16)

    score_high, score_low = repeated(score)
    lane = iota((1, 128), 1) % TOK
    valid = jnp.zeros((1, 128), F32)
    for j in range(TOK):
        valid = jnp.where(lane == j, mask_s[S * TOK + j].astype(F32), valid)
    wait_recv(pin_tile, PAIR_IN)
    pin_scr[...] = pin_tile[...].reshape(TOK * TOK, 128).astype(F32)
    pin = jnp.concatenate([pin_scr[pl.ds(j, TOK, stride=TOK), :] for j in range(TOK)], axis=0)

    half = pl.ds(core * (N // 2), N // 2)
    other = pl.ds((1 - core) * (N // 2), N // 2)
    wait_recv(r_all.at[half], RIGHT)
    remote(r_all.at[half], r_all.at[half], RIGHT_SIB, S, sibling).start()

    def factors_of(ref, part):
        return jnp.concatenate([ref[part, g].reshape(N // 2 * SEQ, 128) for g in range(4)], axis=1)

    wait_recv(l_all, LEFT)
    outer = matmul_tn(factors_of(l_all, half), factors_of(r_all, half))
    wait_recv(r_all.at[other], RIGHT_SIB)
    outer += matmul_tn(factors_of(l_all, other), factors_of(r_all, other))
    for g in range(4):
        o_scr[g] = outer[:, g * 128 : (g + 1) * 128]

    @pl.loop(0, 8, unroll=True)
    def _(cg):
        parts = [
            jnp.concatenate([o_scr[g, pl.ds(4 * cg + q, TOK, stride=32), :] for g in range(4)], axis=0)
            for q in range(4)
        ]
        parts = swap_blocks(parts, 32)
        lanes = pl.ds(pl.multiple_of(cg * 128, 128), 128)
        for j in range(TOK):
            p_scr[pl.ds(j * TOK, TOK), lanes] = parts[j % 4][(j // 4) * TOK : (j // 4 + 1) * TOK]

    p_high, p_low = split(p_scr[...])
    product = matmul(p_high, m_hl[...])
    update = product[:, :128] + (product[:, 128:] + matmul(p_low, m_hl[:, :128]))
    pair_tile = (pin + update).astype(BF16).astype(F32)
    normal = normalize(pair_tile)[0]
    n_high, n_low = split(normal)
    logits = matmul(n_high, score_high) + (matmul(n_high, score_low) + matmul(n_low, score_high))
    own = iota((TOK, 1, 128), 2) % TOK == iota((TOK, 1, 128), 0)
    logits = jnp.sum(jnp.where(own, logits.reshape(TOK, TOK, 128), 0.0), axis=0)
    lg_src[...] = jnp.where(valid > 0, logits, LOW)

    def send_plane(src, dst, phase):
        for d in FAR_FIRST:
            remote(src, dst, phase, plane(d), T).start()
        local(src, dst, phase)

    send_plane(lg_src, lg_all.at[slot(S)], LOGITS)

    po_scr[...] = pair_tile
    for i in range(TOK):
        po_tile[i] = po_scr[pl.ds(i, TOK, stride=TOK), :].astype(BF16)

    @pl.when(y == col)
    def _():
        local(po_tile, po_mid, TURN)

    @pl.when(y != col)
    def _():
        remote(po_tile, po_mid, TURN, col * NC + xpos, row * NC + y).start()

    chip = T // 2

    def place(d, swap=0):
        c = core + swap - 2 * swap * core
        return c * (N // 2) + (chip + d) % (N // 2)

    wait_recv(nv.at[pl.ds(0, 5)], NORM)
    for d, far in ((6, 2), (6, 1), (2, 7)):
        block = nv.at[place(d)]
        remote(block, block, FAR, S, (T + 2 * far) % N).start()
    near = (0, 1, 2, 6, 7)
    for d in near:
        block = nv.at[place(d)]
        remote(block, block, NORM_SIB, S, sibling).start()

    wait_recv(po_mid, TURN)
    top, low = pl.ds(0, TOK // 2), pl.ds(TOK // 2, TOK // 2)
    across_x = pl.ds(xpos * TOK, TOK)
    own_a, own_b = po_all.at[y, top, across_x, :], po_all.at[y, low, across_x, :]
    local(po_mid.at[top], own_a, A1)
    local(po_mid.at[low], own_b, B1)
    for d in (1, 3, 2):
        remote(po_mid.at[top], own_a, A1, y * NC + (xpos + d) % NC, T).start()
        remote(po_mid.at[low], own_b, B1, (S + NC * d) % N, T).start()

    def values(blocks):
        for first in range(0, len(blocks), 2):
            pair = blocks[first : first + 2]
            rows = jnp.concatenate([nv[n].reshape(8 * TOK, 256) for n in pair], axis=0)
            found = matmul(rows, wc_blk[...]).astype(BF16)
            for k, n in enumerate(pair):
                vh[n] = found[k * 128 : (k + 1) * 128].reshape(8, TOK, 1024)

    values([place(d) for d in near])
    wait_recv(nv.at[pl.ds(0, 5)], NORM_SIB)
    values([place(d, 1) for d in near])

    wait_recv(lg_all, LOGITS)
    lg = lg_all[...].reshape(2, 8, TOK, 128)
    parts = swap_blocks([lg[:, s].reshape(2 * TOK, 128) for s in range(8)], TOK)
    lg = jnp.stack([jnp.concatenate([a[:TOK], a[TOK:]], axis=1) for a in parts], axis=0)
    scaled = jnp.exp(lg - jnp.max(lg, axis=-1, keepdims=True))
    prob = scaled / jnp.sum(scaled, axis=-1, keepdims=True)
    prob_scr[...] = prob

    away = (3, 4, 5)
    wait_recv(nv.at[pl.ds(0, 3)], FAR)
    for d in away:
        block = nv.at[place(d)]
        remote(block, block, FAR_SIB, S, sibling).start()
    values([place(d) for d in away])
    wait_recv(nv.at[pl.ds(0, 3)], FAR_SIB)
    values([place(d, 1) for d in away])

    def head(ref, h):
        return [ref[:, g, :, h * 128 : (h + 1) * 128].reshape(256, 128) for g in range(8)]

    gl = []
    for h in range(HEADS):
        gw = matmul_nt(
            jnp.concatenate([gbuf[g * TOK : (g + 1) * TOK, h * 128 : (h + 1) * 128] for g in range(8)], axis=1),
            jnp.concatenate(head(vh, h), axis=1),
        )
        prob = prob_scr[h]
        gl.append(prob * (gw - jnp.sum(prob * gw, axis=-1, keepdims=True)))
    parts = swap_blocks([jnp.concatenate([a[:, :128], a[:, 128:]], axis=0) for a in gl], TOK)
    for s in range(N):
        start = (s % 2) * TOK
        rsbuf[s] = parts[s // 2][start : start + TOK].astype(BF16)
    local(rsbuf.at[S], rsrx.at[S], GL_SUM)

    for d in FAR_FIRST:
        s = plane(d)
        remote(rsbuf.at[s], rsrx.at[S], GL_SUM, s, T).start()

    lines = po_all.at[y, top]
    wait_recv(lines, A1)
    for d in (1, 3, 2):
        remote(lines, lines, A2, (S + NC * d) % N, T).start()
    stripe = po_all.at[:, low, across_x, :]
    wait_recv(stripe, B1)
    for d in (1, 3, 2):
        remote(stripe, stripe, B2, y * NC + (xpos + d) % NC, T).start()

    weights = prob_scr[...].astype(BF16)
    columns = []
    for h in range(HEADS):
        avg = matmul(weights[h], jnp.concatenate(head(vh, h), axis=1))
        avg = jnp.concatenate([avg[:, g * 128 : (g + 1) * 128] for g in range(8)], axis=0)
        columns.append((avg * gate_scr[:, h * 128 : (h + 1) * 128]).astype(BF16))
    mixed = matmul_nt(jnp.concatenate(columns, axis=1), wf_blk[...])
    result = (by_group(x_ref[...].astype(F32)) + mixed).astype(BF16)
    for q in range(4):
        al_scr[:, q] = result[:, q * FEAT : (q + 1) * FEAT].reshape(8, TOK, FEAT)
    al_copy = pltpu.make_async_copy(al_scr, out_al, local_sem.at[10])
    al_copy.start()

    wait_recv(rsrx, GL_SUM)
    gl_tile[...] = jnp.sum(rsrx[...].astype(F32), axis=0).astype(BF16)
    target = gl_all.at[col, xpos]
    owner = row * NC + y

    @pl.when(y == col)
    def _():
        local(gl_tile, target, GL)

    @pl.when(y != col)
    def _():
        remote(gl_tile, target, GL, S, owner).start()

    for d in FAR_FIRST:
        remote(gl_tile, target, GL, plane(d), owner).start()

    wait_recv(po_all.at[pl.ds(0, 3), top], A2)
    wait_recv(po_all.at[pl.ds(0, 3), low], B2)
    po_copy = pltpu.make_async_copy(po_all, out_pair, local_sem.at[9])
    po_copy.start()
    wait_recv(gl_all, GL)
    gl_copy = pltpu.make_async_copy(gl_all, out_gl, local_sem.at[11])
    gl_copy.start()
    al_copy.wait()
    po_copy.wait()

    @pl.when(y == col)
    def _():
        wait_send(pair_hbm.at[pl.ds(0, 3 * TOK), pl.ds(0, TOK), :], PAIR_IN)
        wait_send(rsrx.at[pl.ds(0, 15)], GL)

    @pl.when(y != col)
    def _():
        wait_send(po_tile, TURN)
        wait_send(rsrx, GL)

    @pl.when(alone)
    def _():
        wait_send(r_all.at[pl.ds(0, 7)], RIGHT)

    @pl.when(jnp.logical_not(alone))
    def _():
        wait_send(r_all.at[pl.ds(0, 8)], RIGHT)

    wait_send(l_all.at[pl.ds(0, 15)], LEFT)
    wait_send(r_all.at[pl.ds(0, 8)], RIGHT_SIB)
    wait_send(nv.at[pl.ds(0, 4)], NORM)
    wait_send(nv.at[pl.ds(0, 5)], NORM_SIB)
    wait_send(nv.at[pl.ds(0, 3)], FAR)
    wait_send(nv.at[pl.ds(0, 3)], FAR_SIB)
    wait_send(lg_all.at[pl.ds(0, 15)], LOGITS)
    wait_send(po_all.at[0, pl.ds(0, 8), pl.ds(0, 48), :], A1)
    wait_send(po_all.at[0, pl.ds(0, 8), pl.ds(0, 48), :], B1)
    wait_send(po_all.at[pl.ds(0, 3), top], A2)
    wait_send(po_all.at[pl.ds(0, 3), low], B2)
    wait_send(rsrx.at[pl.ds(0, 15)], GL_SUM)
    gl_copy.wait()


def finish_kernel(
    po_hbm, gl_hbm, score_hbm, al_hbm, out_al, out_pair, out_grad,
    po_ref, gl_ref, score_ref, al_ref, grad_ref, gl_scr, c_hl, sem,
):
    def chunk(ref, n):
        return ref.at[pl.ds(n * TOK, TOK)]

    def load(n):
        return pltpu.make_async_copy(chunk(po_hbm, n), chunk(po_ref, n), sem.at[n])

    def store(n):
        return pltpu.make_async_copy(chunk(grad_ref, n), chunk(out_grad, n), sem.at[NC + n])

    score_copy = pltpu.make_async_copy(score_hbm, score_ref, sem.at[2 * NC])
    gl_copy = pltpu.make_async_copy(gl_hbm, gl_ref, sem.at[2 * NC + 1])
    al_load = pltpu.make_async_copy(al_hbm, al_ref, sem.at[2 * NC + 2])
    al_store = pltpu.make_async_copy(al_ref, out_al, sem.at[2 * NC + 3])

    def keep(n):
        return pltpu.make_async_copy(chunk(po_ref, n), chunk(out_pair, n), sem.at[2 * NC + 4 + n])

    score_copy.start()
    gl_copy.start()
    for n in range(NC):
        load(n).start()
    al_load.start()

    score_copy.wait()
    score = score_ref[...]
    repeat = jnp.where(iota((HEADS, 128), 1) // TOK == iota((HEADS, 128), 0), 1.0, 0.0).astype(BF16)
    high, low = split(score - jnp.mean(score, axis=1, keepdims=True))
    c_hl[:128] = matmul_tn(high, repeat).astype(BF16)
    c_hl[128:] = matmul_tn(low, repeat).astype(BF16)
    gl_copy.wait()
    al_load.wait()
    al_store.start()
    for n in range(NC):
        for s in range(NC):
            gl_scr[n * TOK : (n + 1) * TOK, s] = gl_ref[n, s].astype(F32).reshape(TOK, 1, 128)
    own = (iota((1, 1, TOK, 128), 3) % TOK) == iota((1, 1, TOK, 128), 2)
    part = TOK // 2

    @pl.loop(0, NC)
    def _(n):
        load(n).wait()
        keep(n).start()
        for b in range(2):
            rows = pl.ds(n * TOK + b * part, part)
            normal, inverse = normalize(po_ref[rows].reshape(part * 64, 128).astype(F32))
            lhs = jnp.where(own, gl_scr[rows], 0.0).astype(BF16).reshape(part * 64, 128)
            grad = matmul_nt(lhs, c_hl[...])
            grad = grad[:, :128] + grad[:, 128:]
            along = jnp.mean(grad * normal, axis=-1, keepdims=True)
            grad_ref[rows] = (inverse * (grad - normal * along)).astype(BF16).reshape(part, 64, 128)
        store(n).start()

    for n in range(NC):
        store(n).wait()
        keep(n).wait()
    al_store.wait()


def on_device(
    alignment_input,
    pair_input,
    token_valid_mask,
    first_factor_weights,
    second_factor_weights,
    content_weights_grid,
    sigmoid_weights_grid,
    outer_matrix,
    score_matrix,
    final_mixing_weights,
    adjoint_of_rowset,
):
    smem = pl.BlockSpec(memory_space=pltpu.SMEM)
    hbm = pl.BlockSpec(memory_space=pltpu.HBM)
    V = pltpu.VMEM
    scratch = [
        V((8, 4, TOK, FEAT), BF16),
        V((8, 4, TOK, FEAT), BF16),
        V((32, FEAT), BF16),
        V((32, FEAT), BF16),
        V((FEAT, 256), BF16),
        V((FEAT, 256), BF16),
        V((FEAT, 256), BF16),
        V((HEADS, 128), F32),
        V((1024, 128), F32),
        V((SEQ * TOK, FEAT), F32),
        V((4, SEQ, 128), BF16),
        V((4, SEQ, 128), BF16),
        V((N, 4, SEQ, 128), BF16),
        V((N, 4, SEQ, 128), BF16),
        V((8, TOK, 256), BF16),
        V((N, 8, TOK, 256), BF16),
        V((N, 8, TOK, 1024), BF16),
        V((128, 1024), BF16),
        V((128, 1024), F32),
        V((256, 1024), BF16),
        V((256, 1024), BF16),
        V((1024, 256), BF16),
        V((TOK, TOK, 128), BF16),
        V((TOK * TOK, 128), F32),
        V((4, 512, 128), F32),
        V((256, 1024), F32),
        V((256, 128), F32),
        V((TOK, TOK, 128), BF16),
        V((TOK, TOK, 128), BF16),
        V((NC, TOK, 64, 128), BF16),
        V((TOK, 128), F32),
        V((N, TOK, 128), F32),
        V((HEADS, TOK, 256), F32),
        V((8, 4, TOK, FEAT), BF16),
        V((N, TOK, 128), BF16),
        V((N, TOK, 128), BF16),
        V((TOK, 128), BF16),
        V((NC, NC, TOK, 128), BF16),
        pltpu.SemaphoreType.DMA((PHASES,)),
        pltpu.SemaphoreType.DMA((PHASES,)),
        pltpu.SemaphoreType.DMA((12,)),
    ]
    grouped = (8, 4, TOK, FEAT)
    aligned, pair_block, grad_logits = pl.pallas_call(
        kernel,
        out_shape=[
            jax.ShapeDtypeStruct(grouped, BF16),
            jax.ShapeDtypeStruct((NC, TOK, 64, 128), BF16),
            jax.ShapeDtypeStruct((NC, NC, TOK, 128), BF16),
        ],
        in_specs=[smem] + [hbm] * 10,
        out_specs=[hbm, hbm, hbm],
        scratch_shapes=scratch,
        compiler_params=pltpu.CompilerParams(
            collective_id=0, has_side_effects=True, vmem_limit_bytes=60 * 1024 * 1024
        ),
        name="msa_block",
    )(
        token_valid_mask,
        alignment_input.reshape(grouped),
        adjoint_of_rowset.reshape(grouped),
        first_factor_weights.T,
        second_factor_weights.T,
        content_weights_grid,
        sigmoid_weights_grid,
        final_mixing_weights.T,
        score_matrix.T,
        outer_matrix,
        pair_input,
    )
    aligned, pair_output, pair_gradient = pl.pallas_call(
        finish_kernel,
        out_shape=[
            jax.ShapeDtypeStruct(grouped, BF16),
            jax.ShapeDtypeStruct((64, 64, 128), BF16),
            jax.ShapeDtypeStruct((64, 64, 128), BF16),
        ],
        in_specs=[hbm] * 4,
        out_specs=[hbm] * 3,
        scratch_shapes=[
            V((64, 64, 128), BF16),
            V((NC, NC, TOK, 128), BF16),
            V((HEADS, 128), F32),
            V(grouped, BF16),
            V((64, 64, 128), BF16),
            V((64, NC, 1, 128), F32),
            V((256, 128), BF16),
            pltpu.SemaphoreType.DMA((3 * NC + 4,)),
        ],
        compiler_params=pltpu.CompilerParams(vmem_limit_bytes=60 * 1024 * 1024),
        name="pair_gradient",
    )(pair_block.reshape(64, 64, 128), grad_logits, score_matrix.T, aligned)
    return aligned.reshape(SEQ, TOK, FEAT), pair_output, pair_gradient


def solution(mesh):
    in_specs = (
        P("seq", ("row", "col"), None),
        P("row", "col", None),
        P(),
        P(),
        P(),
        P(),
        P(),
        P(),
        P(),
        P(),
        P("seq", ("row", "col"), None),
    )
    out_specs = (P("seq", ("row", "col"), None), P("row", "col", None), P("row", "col", None))
    return jax.shard_map(
        on_device, mesh=mesh, in_specs=in_specs, out_specs=out_specs, check_vma=False
    )
```
